128 devices in a mesh: dp: 4 (over y_lo, core), seq: 32 (over x, y_hi, z).
Axes of the slice: x: 4, y: 4 (y_hi: 2, y_lo: 2; y = y_hi * 2 + y_lo), z: 4, core: 2. Of those that a mesh axis runs over, the one named last changes fastest.
Arguments:
- siblings: int32 [4, 64, 16], P('dp', 'seq'), may hold values from 0 to 63, all different within a row
- queries: bfloat16 [4, 64, 512, 2560], P('dp', 'seq'), may hold values from -6 to 6
- grad_out: bfloat16 [4, 64, 512, 2560], P('dp', 'seq'), may hold values from -6 to 6
- keys_in: bfloat16 [4, 64, 16, 512], P('dp', 'seq'), may hold values from -4 to 4
- input_values: bfloat16 [4, 64, 16, 512], P('dp', 'seq'), may hold values from -6 to 6
- summary: bfloat16 [4, 64, 16, 5120], P('dp', 'seq'), may hold values from -6 to 6
Outputs:
- query_gradient: bfloat16 [4, 64, 512, 2560], P('dp', 'seq')
- kv_weight_grad: float32 [5120, 1024], P(('dp', 'seq'))
The draws below stay inside these ranges and needn't reach their ends.
Inputs may be any that keep to these rules, and one draw needn't show every extreme that they name: `siblings`: the 16 entries of one completion's list are distinct completions of the same prompt.
All inputs are finite; a program needn't handle non-finite values.
Results may differ from the reference program's by a relative error of at most 0.012.
Values may be sent and summed in bfloat16 or wider, within the bound.
A program may use at most 192 MiB of HBM per device.

```python
import math
import jax
import jax.numpy as jnp
from jax import lax

D = 5120
QUERY_HEADS = 20
KEY_VALUE_HEADS = 4
HEAD_SIZE = 128
SIB = 16
TQ = 512
SHARED_ROWS = 16
COMPLETION_COUNT = 64
PROMPT_COUNT = 4


def draw_queries(key, part):
    draw_key = jax.random.fold_in(key, 11)
    span_length = (PROMPT_COUNT, COMPLETION_COUNT, TQ, QUERY_HEADS * HEAD_SIZE)
    drawn = jnp.clip(jax.random.normal(draw_key, span_length, jnp.float32), -6.0, 6.0)
    return drawn.astype(jnp.bfloat16)


def draw_keys_in(key, part):
    draw_key = jax.random.fold_in(key, 13)
    span_length = (PROMPT_COUNT, COMPLETION_COUNT, SHARED_ROWS, KEY_VALUE_HEADS * HEAD_SIZE)
    drawn = jnp.clip(jax.random.normal(draw_key, span_length, jnp.float32), -4.0, 4.0)
    return drawn.astype(jnp.bfloat16)


def shard_levels(own_key, shape, pieces, smallest, top_value):
    gain = 1.0
    for axis_at, shards_of in pieces:
        steps = jax.random.uniform(jax.random.fold_in(jax.random.fold_in(own_key, 6), axis_at), (shards_of,), jnp.float32, smallest / len(pieces), top_value / len(pieces))
        gain = gain * jnp.repeat(jnp.exp(steps), shape[axis_at] // shards_of).reshape((-1,) + (1,) * (len(shape) - 1 - axis_at))
    return gain


def distinct(stream_key, rows, number_of, top, lift):
    ranking = jax.random.permutation(jax.random.fold_in(stream_key, 1), number_of)
    favour = ranking
    for power in range(3):
        favour = favour * favour // number_of
    favour = favour * lift // number_of
    tickets = jax.random.randint(jax.random.fold_in(stream_key, 2), (rows, number_of), 0, 4096) + favour
    fixed_rows = jax.random.permutation(jax.random.fold_in(stream_key, 3), rows)[jnp.arange(number_of) % rows]
    tickets = jnp.where(jnp.arange(rows)[:, None] == fixed_rows[None, :], 1 << 14, tickets)
    merit = tickets * number_of + jnp.arange(number_of)
    return lax.top_k(merit.astype(jnp.int32), top)[1].astype(jnp.int32)


def scatter_about(stream_key, dims, width, limit, pieces=(), kind=jnp.bfloat16):
    gain = shard_levels(stream_key, dims, pieces, -0.22, 0.18) if pieces else 1.0
    values = jax.random.normal(stream_key, dims, jnp.float32) * width * gain
    return jnp.minimum(jnp.maximum(values, -limit), limit).astype(kind)


def setup_inputs(seed: int = 0) -> dict:
    key_list = jax.random.split(jax.random.key(seed), 7)
    return {
        "siblings": distinct(key_list[0], PROMPT_COUNT * COMPLETION_COUNT, COMPLETION_COUNT, SIB, 4096).reshape((PROMPT_COUNT, COMPLETION_COUNT, SIB)),
        "queries": draw_queries(jax.random.fold_in(key_list[6], 71), 0),
        "grad_out": scatter_about(key_list[2], (PROMPT_COUNT, COMPLETION_COUNT, TQ, QUERY_HEADS * HEAD_SIZE), 1.0, 6.0, ((0, 4), (1, 32))),
        "keys_in": draw_keys_in(jax.random.fold_in(key_list[6], 71), 0),
        "input_values": scatter_about(key_list[4], (PROMPT_COUNT, COMPLETION_COUNT, SHARED_ROWS, KEY_VALUE_HEADS * HEAD_SIZE), 1.0, 6.0, ((0, 4), (1, 32))),
        "summary": scatter_about(key_list[5], (PROMPT_COUNT, COMPLETION_COUNT, SHARED_ROWS, D), 1.0, 6.0, ((0, 4), (1, 32))),
    }


def attend(query_tile_block, incoming_gradient, key_tile_block, value_tile_block):
    row_length = query_tile_block.shape[0]
    scaling = 1.0 / math.sqrt(HEAD_SIZE)
    query_float = query_tile_block.reshape(row_length, KEY_VALUE_HEADS, QUERY_HEADS // KEY_VALUE_HEADS, HEAD_SIZE).astype(jnp.float32)
    incoming_float = incoming_gradient.reshape(row_length, KEY_VALUE_HEADS, QUERY_HEADS // KEY_VALUE_HEADS, HEAD_SIZE).astype(jnp.float32)
    keys_float = key_tile_block.reshape(-1, KEY_VALUE_HEADS, HEAD_SIZE).astype(jnp.float32)
    values_float = value_tile_block.reshape(-1, KEY_VALUE_HEADS, HEAD_SIZE).astype(jnp.float32)
    scores = jnp.einsum('tgrd,lgd->grtl', query_float, keys_float) * scaling
    largest = lax.optimization_barrier(jnp.max(scores, axis=-1, keepdims=True))
    exponent = jnp.exp(scores - largest)
    probability = exponent / lax.optimization_barrier(jnp.sum(exponent, axis=-1, keepdims=True))
    prob_half = lax.optimization_barrier(probability.astype(jnp.bfloat16)).astype(jnp.float32)
    attended = jnp.einsum('grtl,lgd->grtd', prob_half, values_float)
    upstream_t = jnp.transpose(incoming_float, (1, 2, 0, 3))
    row_delta = lax.optimization_barrier(jnp.sum(upstream_t * attended, axis=-1, keepdims=True))
    prob_grad = jnp.einsum('grtd,lgd->grtl', upstream_t, values_float)
    score_grad = probability * (prob_grad - row_delta)
    score_half = lax.optimization_barrier(score_grad.astype(jnp.bfloat16)).astype(jnp.float32)
    query_gradient = jnp.einsum('grtl,lgd->tgrd', score_half, keys_float) * scaling
    key_gradient = jnp.einsum('grtl,tgrd->lgd', score_half, query_float) * scaling
    value_gradient = jnp.einsum('grtl,grtd->lgd', prob_half, upstream_t)
    return (query_gradient.reshape(row_length, QUERY_HEADS * HEAD_SIZE).astype(jnp.bfloat16), key_gradient.reshape(-1, KEY_VALUE_HEADS * HEAD_SIZE), value_gradient.reshape(-1, KEY_VALUE_HEADS * HEAD_SIZE))

def reference(siblings, queries, grad_out, keys_in, input_values, summary):
    key_value_width = KEY_VALUE_HEADS * HEAD_SIZE
    query_grads = []
    weight_total = jnp.zeros((D, 2 * key_value_width), jnp.float32)
    for prompt in range(PROMPT_COUNT):
        sibling = siblings[prompt]

        def per_member(member):
            chosen = sibling[member]
            key_tile_block = keys_in[prompt][chosen].reshape(SIB * SHARED_ROWS, key_value_width)
            value_tile_block = input_values[prompt][chosen].reshape(SIB * SHARED_ROWS, key_value_width)
            return attend(queries[prompt, member], grad_out[prompt, member], key_tile_block, value_tile_block)
        query_gradient, key_parts, value_parts = lax.map(per_member, jnp.arange(COMPLETION_COUNT, dtype=jnp.int32))
        owners = sibling.reshape(-1).astype(jnp.int32)
        key_total = jnp.zeros((COMPLETION_COUNT, SHARED_ROWS, key_value_width), jnp.float32).at[owners].add(key_parts.reshape(COMPLETION_COUNT * SIB, SHARED_ROWS, key_value_width))
        value_total = jnp.zeros((COMPLETION_COUNT, SHARED_ROWS, key_value_width), jnp.float32).at[owners].add(value_parts.reshape(COMPLETION_COUNT * SIB, SHARED_ROWS, key_value_width))
        grads_half = jnp.concatenate([key_total.astype(jnp.bfloat16), value_total.astype(jnp.bfloat16)], axis=-1).reshape(COMPLETION_COUNT * SHARED_ROWS, 2 * key_value_width)
        hidden = summary[prompt].reshape(COMPLETION_COUNT * SHARED_ROWS, D)
        weight_total = weight_total + jnp.dot(hidden.T, grads_half, preferred_element_type=jnp.float32)
        query_grads.append(query_gradient)
    return (jnp.stack(query_grads), weight_total)
```

```python
import functools
import math

import jax
import jax.numpy as jnp
from jax import lax
from jax.experimental import pallas as pl
from jax.experimental.pallas import tpu as pltpu
from jax.sharding import PartitionSpec as P

HEAD = 128
MESH = pl.DeviceIdType.MESH
LIMIT = 56 * 1024 * 1024


def signal_peers(barrier, axis, me, count):
    def one(i, carry):
        pl.semaphore_signal(
            barrier,
            inc=1,
            device_id={axis: lax.rem(me + i, count)},
            device_id_type=MESH,
        )
        return carry

    lax.fori_loop(1, count, one, 0)


def wait_bytes(ref, count, sem):
    part = ref.at[pl.ds(0, count)]
    pltpu.make_async_copy(part, part, sem).wait()


def gather_kernel(
    n_seq, n_dp, k_ref, v_ref, s_ref, kv_out, s_out, kv_local, local_sem, send_sem, recv_sem
):
    me = lax.axis_index("seq")
    barrier = pltpu.get_barrier_semaphore()
    signal_peers(barrier, "seq", me, n_seq)
    groups = k_ref.shape[1] // HEAD
    for g in range(groups):
        kv_local[:, 2 * g * HEAD : (2 * g + 1) * HEAD] = k_ref[:, g * HEAD : (g + 1) * HEAD]
        kv_local[:, (2 * g + 1) * HEAD : (2 * g + 2) * HEAD] = v_ref[:, g * HEAD : (g + 1) * HEAD]
    pl.semaphore_wait(barrier, n_seq - 1)
    own_kv = pltpu.make_async_copy(kv_local, kv_out.at[me], local_sem.at[0])
    own_s = pltpu.make_async_copy(s_ref.at[me], s_out.at[me], local_sem.at[1])
    own_kv.start()
    own_s.start()

    def push(i, carry):
        peer = lax.rem(me + i, n_seq)
        pltpu.make_async_remote_copy(
            src_ref=kv_local,
            dst_ref=kv_out.at[me],
            send_sem=send_sem.at[0],
            recv_sem=recv_sem.at[0],
            device_id={"seq": peer},
            device_id_type=MESH,
        ).start()
        return carry

    lax.fori_loop(1, n_seq, push, 0)

    def push_summary(i, carry):
        peer = lax.rem(me + i, n_seq)
        pltpu.make_async_remote_copy(
            src_ref=s_ref.at[peer],
            dst_ref=s_out.at[me],
            send_sem=send_sem.at[1],
            recv_sem=recv_sem.at[1],
            device_id={"seq": peer},
            device_id_type=MESH,
        ).start()
        return carry

    lax.fori_loop(1, n_seq, push_summary, 0)
    own_kv.wait()
    own_s.wait()
    wait_bytes(kv_out, n_seq - 1, recv_sem.at[0])
    wait_bytes(s_out, n_seq - 1, recv_sem.at[1])
    wait_bytes(kv_out, n_seq - 1, send_sem.at[0])
    wait_bytes(s_out, n_seq - 1, send_sem.at[1])


def attention_kernel(
    siblings, q_ref, do_ref, kv_ref, dq_ref, part_ref, k_rows, v_rows, dk_acc, dv_acc, acc
):
    own = pl.program_id(1)
    span = kv_ref.shape[1]
    listed = k_rows.shape[0] // span
    heads = q_ref.shape[3] // HEAD
    scale = 1.0 / math.sqrt(HEAD)
    power = scale * math.log2(math.e)
    for j in range(listed):
        s = siblings[own * listed + j]
        k_rows[j * span : (j + 1) * span, :] = kv_ref[s, :, :HEAD]
        v_rows[j * span : (j + 1) * span, :] = kv_ref[s, :, HEAD:]
    keys = k_rows[...]
    values = v_rows[...]
    keys_t = keys.T
    for r in range(heads):
        cols = slice(r * HEAD, (r + 1) * HEAD)
        q = q_ref[0, 0, :, cols]
        do = do_ref[0, 0, :, cols]
        across = (((1,), (1,)), ((), ()))
        scores = lax.dot_general(keys, q, across, preferred_element_type=jnp.float32)
        prob_grad = lax.dot_general(values, do, across, preferred_element_type=jnp.float32)
        largest = jnp.max(scores, axis=0, keepdims=True)
        exponent = jnp.exp2((scores - largest) * power)
        prob = exponent * (1.0 / jnp.sum(exponent, axis=0, keepdims=True))
        prob_half = prob.astype(jnp.bfloat16)
        delta = jnp.sum(prob * prob_grad, axis=0, keepdims=True)
        score_half = (prob * (prob_grad - delta)).astype(jnp.bfloat16)
        dv = jnp.dot(prob_half, do, preferred_element_type=jnp.float32)
        dk = jnp.dot(score_half, q, preferred_element_type=jnp.float32)
        dq_t = jnp.dot(keys_t, score_half, preferred_element_type=jnp.float32)
        dq_ref[0, 0, :, cols] = (dq_t * scale).astype(jnp.bfloat16).T
        if r == 0:
            dk_acc[...] = dk
            dv_acc[...] = dv
        else:
            dk_acc[...] += dk
            dv_acc[...] += dv

    @pl.when(own == 0)
    def _():
        acc[...] = jnp.zeros_like(acc)

    for j in range(listed):
        s = siblings[own * listed + j]
        acc[s, :, :HEAD] += dk_acc[j * span : (j + 1) * span, :] * scale
        acc[s, :, HEAD:] += dv_acc[j * span : (j + 1) * span, :]

    @pl.when(own == pl.num_programs(1) - 1)
    def _():
        part_ref[...] = acc[...].astype(jnp.bfloat16)


def weight_kernel(
    n_seq,
    n_dp,
    part_ref,
    s_ref,
    out_ref,
    terms,
    own_half,
    halves,
    product,
    shares,
    send_sem,
    recv_sem,
    local_sem,
):
    me = lax.axis_index("seq")
    me_dp = lax.axis_index("dp")
    barrier = pltpu.get_barrier_semaphore()
    signal_peers(barrier, "seq", me, n_seq)
    signal_peers(barrier, "dp", me_dp, n_dp)
    pl.semaphore_wait(barrier, n_seq + n_dp - 2)
    own = pltpu.make_async_copy(part_ref.at[me], terms.at[me], local_sem.at[0])
    own.start()

    def push_terms(i, carry):
        peer = lax.rem(me + i, n_seq)
        pltpu.make_async_remote_copy(
            src_ref=part_ref.at[peer],
            dst_ref=terms.at[me],
            send_sem=send_sem.at[0],
            recv_sem=recv_sem.at[0],
            device_id={"seq": peer},
            device_id_type=MESH,
        ).start()
        return carry

    lax.fori_loop(1, n_seq, push_terms, 0)
    own.wait()
    wait_bytes(terms, n_seq - 1, recv_sem.at[0])

    def add(i, total):
        return total + terms[i].astype(jnp.float32)

    total = lax.fori_loop(1, n_seq, add, terms[0].astype(jnp.float32))
    own_half[...] = total.astype(jnp.bfloat16)
    own = pltpu.make_async_copy(own_half, halves.at[me], local_sem.at[0])
    own.start()

    def push_half(i, carry):
        peer = lax.rem(me + i, n_seq)
        pltpu.make_async_remote_copy(
            src_ref=own_half,
            dst_ref=halves.at[me],
            send_sem=send_sem.at[1],
            recv_sem=recv_sem.at[1],
            device_id={"seq": peer},
            device_id_type=MESH,
        ).start()
        return carry

    lax.fori_loop(1, n_seq, push_half, 0)
    own.wait()
    wait_bytes(halves, n_seq - 1, recv_sem.at[1])
    rows = n_seq * halves.shape[1]
    hidden = s_ref[...].reshape(rows, s_ref.shape[2])
    grads = halves[...].reshape(rows, halves.shape[2])
    product[...] = lax.dot_general(
        hidden, grads, (((0,), (0,)), ((), ())), preferred_element_type=jnp.float32
    ).reshape(product.shape)

    def push_share(i, carry):
        peer = lax.rem(me_dp + i, n_dp)
        pltpu.make_async_remote_copy(
            src_ref=product.at[peer],
            dst_ref=shares.at[me_dp],
            send_sem=send_sem.at[2],
            recv_sem=recv_sem.at[2],
            device_id={"dp": peer},
            device_id_type=MESH,
        ).start()
        return carry

    lax.fori_loop(1, n_dp, push_share, 0)
    own = pltpu.make_async_copy(product.at[me_dp], shares.at[me_dp], local_sem.at[0])
    own.start()
    own.wait()
    wait_bytes(shares, n_dp - 1, recv_sem.at[2])
    result = shares[0]
    for d in range(1, n_dp):
        result = result + shares[d]
    half = out_ref.shape[1] // 2
    for g in range(half // HEAD):
        out_ref[:, g * HEAD : (g + 1) * HEAD] = result[:, 2 * g * HEAD : (2 * g + 1) * HEAD]
        out_ref[:, half + g * HEAD : half + (g + 1) * HEAD] = result[
            :, (2 * g + 1) * HEAD : (2 * g + 2) * HEAD
        ]
    wait_bytes(terms, n_seq - 1, send_sem.at[0])
    wait_bytes(halves, n_seq - 1, send_sem.at[1])
    wait_bytes(shares, n_dp - 1, send_sem.at[2])


def per_device(n_dp, n_seq, siblings, queries, grad_out, keys_in, input_values, summary):
    _, own, tokens, q_width = queries.shape
    span, kv_width = keys_in.shape[2], keys_in.shape[3]
    listed = siblings.shape[2]
    groups = kv_width // HEAD
    rows = own * span
    everyone = n_seq * own
    width = summary.shape[3]
    block = width // (n_dp * n_seq)
    any_space = pl.BlockSpec(memory_space=pl.ANY)
    vmem = pl.BlockSpec(memory_space=pltpu.VMEM)
    pieces = (
        summary.reshape(rows, n_dp, n_seq, block)
        .transpose(2, 0, 1, 3)
        .reshape(n_seq, rows, n_dp * block)
    )
    kv_all, hidden = pl.pallas_call(
        functools.partial(gather_kernel, n_seq, n_dp),
        out_shape=(
            jax.ShapeDtypeStruct((n_seq, rows, 2 * kv_width), jnp.bfloat16),
            jax.ShapeDtypeStruct((n_seq, rows, n_dp * block), jnp.bfloat16),
        ),
        in_specs=[vmem, vmem, any_space],
        out_specs=(any_space, any_space),
        scratch_shapes=[
            pltpu.VMEM((rows, 2 * kv_width), jnp.bfloat16),
            pltpu.SemaphoreType.DMA((2,)),
            pltpu.SemaphoreType.DMA((2,)),
            pltpu.SemaphoreType.DMA((2,)),
        ],
        compiler_params=pltpu.CompilerParams(
            collective_id=0, has_side_effects=True, vmem_limit_bytes=LIMIT
        ),
    )(keys_in.reshape(rows, kv_width), input_values.reshape(rows, kv_width), pieces)
    kv_all = kv_all.reshape(everyone, span, 2 * kv_width)
    q_block = q_width // groups
    token_spec = pl.BlockSpec((1, 1, tokens, q_block), lambda g, c, s: (0, c, 0, g))
    dq, part = pl.pallas_call(
        attention_kernel,
        grid_spec=pltpu.PrefetchScalarGridSpec(
            num_scalar_prefetch=1,
            grid=(groups, own),
            in_specs=[
                token_spec,
                token_spec,
                pl.BlockSpec((everyone, span, 2 * HEAD), lambda g, c, s: (0, 0, g)),
            ],
            out_specs=[
                token_spec,
                pl.BlockSpec((everyone, span, 2 * HEAD), lambda g, c, s: (0, 0, g)),
            ],
            scratch_shapes=[
                pltpu.VMEM((listed * span, HEAD), jnp.bfloat16),
                pltpu.VMEM((listed * span, HEAD), jnp.bfloat16),
                pltpu.VMEM((listed * span, HEAD), jnp.float32),
                pltpu.VMEM((listed * span, HEAD), jnp.float32),
                pltpu.VMEM((everyone, span, 2 * HEAD), jnp.float32),
            ],
        ),
        out_shape=(
            jax.ShapeDtypeStruct(queries.shape, jnp.bfloat16),
            jax.ShapeDtypeStruct((everyone, span, 2 * kv_width), jnp.bfloat16),
        ),
        compiler_params=pltpu.CompilerParams(vmem_limit_bytes=LIMIT),
    )(siblings.reshape(-1), queries, grad_out, kv_all)
    weight_grad = pl.pallas_call(
        functools.partial(weight_kernel, n_seq, n_dp),
        out_shape=jax.ShapeDtypeStruct((block, 2 * kv_width), jnp.float32),
        in_specs=[any_space, vmem],
        out_specs=vmem,
        scratch_shapes=[
            pltpu.VMEM((n_seq, rows, 2 * kv_width), jnp.bfloat16),
            pltpu.VMEM((rows, 2 * kv_width), jnp.bfloat16),
            pltpu.VMEM((n_seq, rows, 2 * kv_width), jnp.bfloat16),
            pltpu.VMEM((n_dp, block, 2 * kv_width), jnp.float32),
            pltpu.VMEM((n_dp, block, 2 * kv_width), jnp.float32),
            pltpu.SemaphoreType.DMA((3,)),
            pltpu.SemaphoreType.DMA((3,)),
            pltpu.SemaphoreType.DMA((1,)),
        ],
        compiler_params=pltpu.CompilerParams(
            collective_id=1, has_side_effects=True, vmem_limit_bytes=LIMIT
        ),
    )(part.reshape(n_seq, rows, 2 * kv_width), hidden)
    return (dq, weight_grad)


def solution(mesh):
    placed = (
        P("dp", "seq", None),
        P("dp", "seq", None, None),
        P("dp", "seq", None, None),
        P("dp", "seq", None, None),
        P("dp", "seq", None, None),
        P("dp", "seq", None, None),
    )
    return jax.shard_map(
        functools.partial(per_device, mesh.shape["dp"], mesh.shape["seq"]),
        mesh=mesh,
        in_specs=placed,
        out_specs=(P("dp", "seq", None, None), P(("dp", "seq"), None)),
        check_vma=False,
    )
```

```python
import functools
import math

import jax
import jax.numpy as jnp
from jax import lax
from jax.experimental import pallas as pl
from jax.experimental.pallas import tpu as pltpu
from jax.sharding import PartitionSpec as P

HEAD = 128
MESH = pl.DeviceIdType.MESH
RING = 4
SPREAD = 5
REDUCE = 5
LIMIT = 56 * 1024 * 1024


def signal_peers(barrier, axis, me, count):
    def one(i, carry):
        pl.semaphore_signal(
            barrier,
            inc=1,
            device_id={axis: lax.rem(me + i, count)},
            device_id_type=MESH,
        )
        return carry

    lax.fori_loop(1, count, one, 0)


def wait_bytes(ref, count, sem):
    part = ref.at[pl.ds(0, count)]
    pltpu.make_async_copy(part, part, sem).wait()


def ring(at, shift):
    return lax.rem(at + shift + RING, RING)


def place():
    me = lax.axis_index("seq")
    return me // (2 * RING), lax.rem(me // RING, 2), lax.rem(me, RING)


def peer_id(x, y, z):
    return {"seq": (x * 2 + y) * RING + z}


def neighbours():
    x, y, z = place()
    return [
        peer_id(x, 1 - y, z),
        peer_id(ring(x, 1), y, z),
        peer_id(ring(x, -1), y, z),
        peer_id(x, y, ring(z, 1)),
        peer_id(x, y, ring(z, -1)),
    ]


def remote(src, dst, peer, send_sem, recv_sem):
    return pltpu.make_async_remote_copy(
        src_ref=src,
        dst_ref=dst,
        send_sem=send_sem,
        recv_sem=recv_sem,
        device_id=peer,
        device_id_type=MESH,
    )


def spread_copies(buf, g, stage, send_sem, recv_sem):
    x, y, z = place()
    right, left = peer_id(ring(x, 1), y, z), peer_id(ring(x, -1), y, z)
    up, down = peer_id(x, y, ring(z, 1)), peer_id(x, y, ring(z, -1))
    every, both = pl.ds(0, RING), pl.ds(0, 2)
    xl, xr, zd, zu = ring(x, -1), ring(x, 1), ring(z, -1), ring(z, 1)
    moves = [
        [((x, y, z), peer_id(x, 1 - y, z))],
        [
            ((x, both, z, 0), up),
            ((x, both, z, 0), down),
            ((x, both, z, 1), right),
            ((x, both, z, 1), left),
        ],
        [
            ((x, 0, zd, 0), up),
            ((x, 1, zu, 0), down),
            ((xl, 0, z, 1), right),
            ((xr, 1, z, 1), left),
        ],
        [
            ((x, both, every, 0), right),
            ((x, both, every, 0), left),
            ((every, both, z, 1), up),
            ((every, both, z, 1), down),
        ],
        [
            ((xl, 0, every, 0), right),
            ((xr, 1, every, 0), left),
            ((every, 0, zd, 1), up),
            ((every, 1, zu, 1), down),
        ],
    ][stage]
    return [
        remote(
            buf.at[(g, *where)],
            buf.at[(g, *where)],
            peer,
            send_sem.at[g, 4 * stage + i],
            recv_sem.at[g, 4 * stage + i],
        )
        for i, (where, peer) in enumerate(moves)
    ]


def spread(buf, g, stage, send_sem, recv_sem):
    if stage > 0:
        for copy in spread_copies(buf, g, stage - 1, send_sem, recv_sem):
            copy.wait()
    if stage < SPREAD:
        for copy in spread_copies(buf, g, stage, send_sem, recv_sem):
            copy.start()


def reduce_copies(part, slots, g, stage, send_sem, recv_sem):
    x, y, z = place()
    right, left = peer_id(ring(x, 1), y, z), peer_id(ring(x, -1), y, z)
    up, down = peer_id(x, y, ring(z, 1)), peer_id(x, y, ring(z, -1))
    every, both = pl.ds(0, RING), pl.ds(0, 2)
    xl, xr, x2 = ring(x, -1), ring(x, 1), ring(x, 2)
    zd, zu, z2 = ring(z, -1), ring(z, 1), ring(z, 2)
    if stage == 4:
        moves = [((), peer_id(x, 1 - y, z))]
        source = slots[5]
    else:
        source = part
        moves = [
            [
                ((x2, 0, every, 0), right),
                ((x2, 1, every, 0), left),
                ((every, 0, z2, 1), up),
                ((every, 1, z2, 1), down),
            ],
            [
                ((xr, both, every, 0), right),
                ((xl, both, every, 0), left),
                ((every, both, zu, 1), up),
                ((every, both, zd, 1), down),
            ],
            [
                ((x, 0, z2, 0), up),
                ((x, 1, z2, 0), down),
                ((x2, 0, z, 1), right),
                ((x2, 1, z, 1), left),
            ],
            [
                ((x, both, zu, 0), up),
                ((x, both, zd, 0), down),
                ((xr, both, z, 1), right),
                ((xl, both, z, 1), left),
            ],
        ][stage]
    return [
        remote(
            source.at[(g, *where)],
            landing(slots, stage, i).at[g, i % 2 if stage == 1 else i],
            peer,
            send_sem.at[g, 4 * stage + i],
            recv_sem.at[g, 4 * stage + i],
        )
        for i, (where, peer) in enumerate(moves)
    ]


def landing(slots, stage, i):
    return slots[1][i // 2] if stage == 1 else slots[stage]


def wide(value):
    return value.astype(jnp.float32)


def reduce(part, slots, halves, g, stage, send_sem, recv_sem):
    x, y, z = place()
    every, both = slice(None), slice(None)
    xl, xr, zd, zu = ring(x, -1), ring(x, 1), ring(z, -1), ring(z, 1)
    if stage > 0:
        for copy in reduce_copies(part, slots, g, stage - 1, send_sem, recv_sem):
            copy.wait()
        came = slots[stage - 1]

        def add(where, i):
            at = (g, *where)
            part[at] = (wide(part[at]) + wide(came[g, i])).astype(part.dtype)

        def three(where, term):
            total = wide(part[(g, *where)]) + wide(term[g, 0]) + wide(term[g, 1])
            part[(g, *where)] = total.astype(part.dtype)

        if stage == 1:
            add((xr, 0, every, 0), 0)
            add((xl, 1, every, 0), 1)
            add((every, 0, zu, 1), 2)
            add((every, 1, zd, 1), 3)
        elif stage == 2:
            three((x, both, every, 0), came[0])
            three((every, both, z, 1), came[1])
        elif stage == 3:
            add((x, 0, zu, 0), 0)
            add((x, 1, zd, 0), 1)
            add((xr, 0, z, 1), 2)
            add((xl, 1, z, 1), 3)
        elif stage == 4:
            for half, first in ((0, 0), (1, 2)):
                for at, total in ((1 - y, slots[5]), (y, slots[6])):
                    total[g, half] = (
                        wide(part[g, x, at, z, half])
                        + wide(came[g, first, at])
                        + wide(came[g, first + 1, at])
                    )
        else:
            halves[g, x, y, z] = (slots[6][g] + came[g, 0]).astype(halves.dtype)
    if stage < REDUCE:
        for copy in reduce_copies(part, slots, g, stage, send_sem, recv_sem):
            copy.start()


def reduce_slots(groups, span, wide_cols, kind):
    row = (span, wide_cols)
    return [
        pltpu.VMEM((groups, 4, RING, *row), kind),
        pltpu.VMEM((groups, 2, 2, RING, *row), kind),
        pltpu.VMEM((groups, 2, RING, 2, *row), kind),
        pltpu.VMEM((groups, 4, *row), kind),
        pltpu.VMEM((groups, 4, 2, *row), kind),
        pltpu.VMEM((groups, 1, 2, *row), jnp.float32),
        pltpu.VMEM((groups, 2, *row), jnp.float32),
        pltpu.VMEM((groups, 2, *row), jnp.float32),
    ]


def wavefront(groups, stages, step):
    for d in range(groups + stages):
        for g in range(groups):
            if 0 <= d - g <= stages:
                step(g, d - g)


def gather_kernel(
    n_seq, k_ref, v_ref, s_ref, kv_out, s_out, kv, local_sem, send_sem, recv_sem, s_send, s_recv
):
    me = lax.axis_index("seq")
    x, y, z = place()
    barrier = pltpu.get_barrier_semaphore()
    signal_peers(barrier, "seq", me, n_seq)
    groups = k_ref.shape[2] // HEAD
    for g in range(groups):
        cols = slice(g * HEAD, (g + 1) * HEAD)
        kv[g, x, y, z, :, :, :HEAD] = k_ref[:, :, cols]
        kv[g, x, y, z, :, :, HEAD:] = v_ref[:, :, cols]
    pl.semaphore_wait(barrier, n_seq - 1)
    for g in range(groups):
        spread(kv, g, 0, send_sem, recv_sem)
    own_s = pltpu.make_async_copy(s_ref.at[me], s_out.at[me], local_sem.at[0])
    own_s.start()

    def push_summary(i, carry):
        peer = lax.rem(me + i, n_seq)
        remote(
            s_ref.at[peer], s_out.at[me], {"seq": peer}, s_send.at[0], s_recv.at[0]
        ).start()
        return carry

    lax.fori_loop(1, n_seq, push_summary, 0)
    wavefront(
        groups, SPREAD - 1, lambda g, stage: spread(kv, g, stage + 1, send_sem, recv_sem)
    )
    done = pltpu.make_async_copy(kv, kv_out, local_sem.at[1])
    done.start()
    own_s.wait()
    wait_bytes(s_out, n_seq - 1, s_recv.at[0])
    wait_bytes(s_out, n_seq - 1, s_send.at[0])
    done.wait()


def attention_kernel(
    siblings, q_ref, do_ref, kv_ref, dq_ref, part_ref, k_rows, v_rows, dk_acc, dv_acc, acc
):
    own = pl.program_id(1)
    span = kv_ref.shape[2]
    listed = k_rows.shape[0] // span
    heads = q_ref.shape[3] // HEAD
    scale = 1.0 / math.sqrt(HEAD)
    power = scale * math.log2(math.e)
    for j in range(listed):
        s = siblings[own * listed + j]
        k_rows[j * span : (j + 1) * span, :] = kv_ref[0, s, :, :HEAD]
        v_rows[j * span : (j + 1) * span, :] = kv_ref[0, s, :, HEAD:]
    keys = k_rows[...]
    values = v_rows[...]
    keys_t = keys.T
    for r in range(heads):
        cols = slice(r * HEAD, (r + 1) * HEAD)
        q = q_ref[0, 0, :, cols]
        do = do_ref[0, 0, :, cols]
        across = (((1,), (1,)), ((), ()))
        scores = lax.dot_general(keys, q, across, preferred_element_type=jnp.float32)
        prob_grad = lax.dot_general(values, do, across, preferred_element_type=jnp.float32)
        largest = jnp.max(scores, axis=0, keepdims=True)
        exponent = jnp.exp2((scores - largest) * power)
        prob = exponent * (1.0 / jnp.sum(exponent, axis=0, keepdims=True))
        prob_half = prob.astype(jnp.bfloat16)
        delta = jnp.sum(prob * prob_grad, axis=0, keepdims=True)
        score_half = (prob * (prob_grad - delta)).astype(jnp.bfloat16)
        dv = jnp.dot(prob_half, do, preferred_element_type=jnp.float32)
        dk = jnp.dot(score_half, q, preferred_element_type=jnp.float32)
        dq_t = jnp.dot(keys_t, score_half, preferred_element_type=jnp.float32)
        dq_ref[0, 0, :, cols] = (dq_t * scale).astype(jnp.bfloat16).T
        if r == 0:
            dk_acc[...] = dk
            dv_acc[...] = dv
        else:
            dk_acc[...] += dk
            dv_acc[...] += dv

    @pl.when(own == 0)
    def _():
        acc[...] = jnp.zeros_like(acc)

    for j in range(listed):
        s = siblings[own * listed + j]
        acc[s, :, :HEAD] += dk_acc[j * span : (j + 1) * span, :] * scale
        acc[s, :, HEAD:] += dv_acc[j * span : (j + 1) * span, :]

    @pl.when(own == pl.num_programs(1) - 1)
    def _():
        part_ref[0] = acc[...].astype(jnp.bfloat16)


def weight_kernel(
    groups,
    n_dp,
    part_ref,
    s_ref,
    out_ref,
    part,
    halves,
    product,
    shares,
    s0,
    s1a,
    s1b,
    s2,
    s3,
    s4,
    s5,
    s6,
    red_send,
    red_recv,
    spr_send,
    spr_recv,
    send_sem,
    recv_sem,
    local_sem,
):
    me_dp = lax.axis_index("dp")
    barrier = pltpu.get_barrier_semaphore()
    for peer in neighbours():
        pl.semaphore_signal(barrier, inc=1, device_id=peer, device_id_type=MESH)
    signal_peers(barrier, "dp", me_dp, n_dp)
    load = pltpu.make_async_copy(part_ref, part, local_sem.at[0])
    load.start()
    pl.semaphore_wait(barrier, 5 + n_dp - 1)
    load.wait()
    slots = (s0, (s1a, s1b), s2, s3, s4, s5, s6)

    def step(g, stage):
        if stage <= REDUCE:
            reduce(part, slots, halves, g, stage, red_send, red_recv)
        if stage >= REDUCE:
            spread(halves, g, stage - REDUCE, spr_send, spr_recv)

    wavefront(groups, REDUCE + SPREAD, step)
    rows = s_ref.shape[0] * s_ref.shape[1]
    hidden = s_ref[...].reshape(rows, s_ref.shape[2])
    for g in range(groups):
        grads = halves[g].reshape(rows, 2 * HEAD)
        got = lax.dot_general(
            hidden, grads, (((0,), (0,)), ((), ())), preferred_element_type=jnp.float32
        ).reshape(product.shape[0], product.shape[1], 2 * HEAD)
        product[:, :, g * HEAD : (g + 1) * HEAD] = got[:, :, :HEAD]
        product[:, :, (groups + g) * HEAD : (groups + g + 1) * HEAD] = got[:, :, HEAD:]

    def push_share(i, carry):
        peer = lax.rem(me_dp + i, n_dp)
        remote(
            product.at[peer], shares.at[me_dp], {"dp": peer}, send_sem.at[0], recv_sem.at[0]
        ).start()
        return carry

    lax.fori_loop(1, n_dp, push_share, 0)
    shares[me_dp] = product[me_dp]
    wait_bytes(shares, n_dp - 1, recv_sem.at[0])
    result = shares[0]
    for d in range(1, n_dp):
        result = result + shares[d]
    out_ref[...] = result
    wait_bytes(shares, n_dp - 1, send_sem.at[0])


def per_device(n_dp, n_seq, siblings, queries, grad_out, keys_in, input_values, summary):
    _, own, tokens, q_width = queries.shape
    span, kv_width = keys_in.shape[2], keys_in.shape[3]
    listed = siblings.shape[2]
    groups = kv_width // HEAD
    rows = own * span
    everyone = n_seq * own
    width = summary.shape[3]
    block = width // (n_dp * n_seq)
    any_space = pl.BlockSpec(memory_space=pl.ANY)
    vmem = pl.BlockSpec(memory_space=pltpu.VMEM)
    pieces = (
        summary.reshape(rows, n_dp, n_seq, block)
        .transpose(2, 0, 1, 3)
        .reshape(n_seq, rows, n_dp * block)
    )
    tile = (RING, 2, RING, own, span, 2 * HEAD)
    kv_all, hidden = pl.pallas_call(
        functools.partial(gather_kernel, n_seq),
        out_shape=(
            jax.ShapeDtypeStruct((groups, *tile), jnp.bfloat16),
            jax.ShapeDtypeStruct((n_seq, rows, n_dp * block), jnp.bfloat16),
        ),
        in_specs=[vmem, vmem, any_space],
        out_specs=(any_space, any_space),
        scratch_shapes=[
            pltpu.VMEM((groups, *tile), jnp.bfloat16),
            pltpu.SemaphoreType.DMA((2,)),
            pltpu.SemaphoreType.DMA((groups, 4 * SPREAD)),
            pltpu.SemaphoreType.DMA((groups, 4 * SPREAD)),
            pltpu.SemaphoreType.DMA((1,)),
            pltpu.SemaphoreType.DMA((1,)),
        ],
        compiler_params=pltpu.CompilerParams(
            collective_id=0, has_side_effects=True, vmem_limit_bytes=LIMIT
        ),
    )(keys_in[0], input_values[0], pieces)
    kv_all = kv_all.reshape(groups, everyone, span, 2 * HEAD)
    q_block = q_width // groups
    token_spec = pl.BlockSpec((1, 1, tokens, q_block), lambda g, c, s: (0, c, 0, g))
    dq, part = pl.pallas_call(
        attention_kernel,
        grid_spec=pltpu.PrefetchScalarGridSpec(
            num_scalar_prefetch=1,
            grid=(groups, own),
            in_specs=[
                token_spec,
                token_spec,
                pl.BlockSpec((1, everyone, span, 2 * HEAD), lambda g, c, s: (g, 0, 0, 0)),
            ],
            out_specs=[
                token_spec,
                pl.BlockSpec((1, everyone, span, 2 * HEAD), lambda g, c, s: (g, 0, 0, 0)),
            ],
            scratch_shapes=[
                pltpu.VMEM((listed * span, HEAD), jnp.bfloat16),
                pltpu.VMEM((listed * span, HEAD), jnp.bfloat16),
                pltpu.VMEM((listed * span, HEAD), jnp.float32),
                pltpu.VMEM((listed * span, HEAD), jnp.float32),
                pltpu.VMEM((everyone, span, 2 * HEAD), jnp.float32),
            ],
        ),
        out_shape=(
            jax.ShapeDtypeStruct(queries.shape, jnp.bfloat16),
            jax.ShapeDtypeStruct((groups, everyone, span, 2 * HEAD), jnp.bfloat16),
        ),
        compiler_params=pltpu.CompilerParams(vmem_limit_bytes=LIMIT),
    )(siblings.reshape(-1), queries, grad_out, kv_all)
    weight_grad = pl.pallas_call(
        functools.partial(weight_kernel, groups, n_dp),
        out_shape=jax.ShapeDtypeStruct((block, 2 * kv_width), jnp.float32),
        in_specs=[any_space, vmem],
        out_specs=vmem,
        scratch_shapes=[
            pltpu.VMEM((groups, *tile), jnp.bfloat16),
            pltpu.VMEM((groups, *tile), jnp.bfloat16),
            pltpu.VMEM((n_dp, block, 2 * kv_width), jnp.float32),
            pltpu.VMEM((n_dp, block, 2 * kv_width), jnp.float32),
            *reduce_slots(groups, span, 2 * HEAD, jnp.bfloat16),
            pltpu.SemaphoreType.DMA((groups, 4 * REDUCE)),
            pltpu.SemaphoreType.DMA((groups, 4 * REDUCE)),
            pltpu.SemaphoreType.DMA((groups, 4 * SPREAD)),
            pltpu.SemaphoreType.DMA((groups, 4 * SPREAD)),
            pltpu.SemaphoreType.DMA((1,)),
            pltpu.SemaphoreType.DMA((1,)),
            pltpu.SemaphoreType.DMA((1,)),
        ],
        compiler_params=pltpu.CompilerParams(
            collective_id=1, has_side_effects=True, vmem_limit_bytes=LIMIT
        ),
    )(part.reshape(groups, *tile), hidden)
    return (dq, weight_grad)


def solution(mesh):
    placed = (
        P("dp", "seq", None),
        P("dp", "seq", None, None),
        P("dp", "seq", None, None),
        P("dp", "seq", None, None),
        P("dp", "seq", None, None),
        P("dp", "seq", None, None),
    )
    return jax.shard_map(
        functools.partial(per_device, mesh.shape["dp"], mesh.shape["seq"]),
        mesh=mesh,
        in_specs=placed,
        out_specs=(P("dp", "seq", None, None), P(("dp", "seq"), None)),
        check_vma=False,
    )
```

```python
import functools
import math

import jax
import jax.numpy as jnp
from jax import lax
from jax.experimental import pallas as pl
from jax.experimental.pallas import tpu as pltpu
from jax.sharding import PartitionSpec as P

HEAD = 128
MESH = pl.DeviceIdType.MESH
LIMIT = 56 * 1024 * 1024
RING = 4
PLANE = 2 * RING


def signal_peers(barrier, axis, me, count):
    def one(i, carry):
        pl.semaphore_signal(
            barrier,
            inc=1,
            device_id={axis: lax.rem(me + i, count)},
            device_id_type=MESH,
        )
        return carry

    lax.fori_loop(1, count, one, 0)


def wait_blocks(ref, count, sem):
    part = ref.at[pl.ds(0, count)]
    pltpu.make_async_copy(part, part, sem).wait()


def wide(value):
    return value.astype(jnp.float32)


def ring(at, shift):
    return lax.rem(at + shift, RING)


def place():
    me = lax.axis_index("seq")
    return me // PLANE, lax.rem(me // RING, 2), lax.rem(me, RING)


def peer_id(x, y, z):
    return {"seq": x * PLANE + y * RING + z}


def remote(src, dst, peer, send_sem, recv_sem):
    return pltpu.make_async_remote_copy(
        src_ref=src,
        dst_ref=dst,
        send_sem=send_sem,
        recv_sem=recv_sem,
        device_id=peer,
        device_id_type=MESH,
    )


def plane_shifts():
    return [(i // RING, i % RING) for i in range(1, PLANE)]


class Spread:
    def __init__(self, buf, ruler, send_sem, recv_sem):
        self.buf, self.ruler = buf, ruler
        self.send_sem, self.recv_sem = send_sem, recv_sem

    def start_plane(self, g):
        x, y, z = place()
        for dy, shift in plane_shifts():
            other = lax.rem(y + dy, 2)
            for half, peer in (
                (0, peer_id(x, other, ring(z, shift))),
                (1, peer_id(ring(x, shift), other, z)),
            ):
                block = self.buf.at[g, x, y, z, half]
                remote(block, block, peer, self.send_sem.at[g, 0], self.recv_sem.at[g, 0]).start()

    def wait_plane(self, g):
        wait_blocks(self.ruler, 2 * (PLANE - 1), self.recv_sem.at[g, 0])

    def start_line(self, g):
        x, y, z = place()
        for shift in (1, 3, 2):
            first = self.buf.at[g, x, :, :, 0]
            second = self.buf.at[g, :, :, z, 1]
            sems = (self.send_sem.at[g, 1], self.recv_sem.at[g, 1])
            remote(first, first, peer_id(ring(x, shift), y, z), *sems).start()
            remote(second, second, peer_id(x, y, ring(z, shift)), *sems).start()

    def wait_line(self, g):
        wait_blocks(self.ruler, 2 * (RING - 1) * PLANE, self.recv_sem.at[g, 1])

    def wait_sent(self, g):
        wait_blocks(self.ruler, 2 * (PLANE - 1), self.send_sem.at[g, 0])
        wait_blocks(self.ruler, 2 * (RING - 1) * PLANE, self.send_sem.at[g, 1])


class Reduce:
    def __init__(self, part, line_a, line_b, sum_a, sum_b, plane, ruler, send_sem, recv_sem):
        self.part, self.ruler = part, ruler
        self.line_a, self.line_b = line_a, line_b
        self.sum_a, self.sum_b, self.plane = sum_a, sum_b, plane
        self.send_sem, self.recv_sem = send_sem, recv_sem

    def start_line(self, g):
        x, y, z = place()
        sems = (self.send_sem.at[g, 0], self.recv_sem.at[g, 0])
        for shift in (1, 3, 2):
            xs, zs = ring(x, shift), ring(z, shift)
            slot = shift - 1
            remote(
                self.part.at[g, xs, :, :, 0], self.line_a.at[g, slot], peer_id(xs, y, z), *sems
            ).start()
            remote(
                self.part.at[g, :, :, zs, 1], self.line_b.at[g, slot], peer_id(x, y, zs), *sems
            ).start()

    def line_to_plane(self, g):
        x, y, z = place()
        wait_blocks(self.ruler, 2 * (RING - 1) * PLANE, self.recv_sem.at[g, 0])
        total_a = wide(self.part[g, x, :, :, 0])
        total_b = wide(self.part[g, :, :, z, 1])
        for slot in range(RING - 1):
            total_a += wide(self.line_a[g, slot])
            total_b += wide(self.line_b[g, slot])
        self.sum_a[g] = total_a.astype(jnp.bfloat16)
        self.sum_b[g] = total_b.astype(jnp.bfloat16)
        sems = (self.send_sem.at[g, 1], self.recv_sem.at[g, 1])
        for i, (dy, shift) in enumerate(plane_shifts()):
            other, xs, zs = lax.rem(y + dy, 2), ring(x, shift), ring(z, shift)
            remote(
                self.sum_a.at[g, other, zs], self.plane.at[g, 0, i], peer_id(x, other, zs), *sems
            ).start()
            remote(
                self.sum_b.at[g, xs, other], self.plane.at[g, 1, i], peer_id(xs, other, z), *sems
            ).start()

    def finish(self, g, out):
        x, y, z = place()
        wait_blocks(self.ruler, 2 * (PLANE - 1), self.recv_sem.at[g, 1])
        for half, own in ((0, self.sum_a[g, y, z]), (1, self.sum_b[g, x, y])):
            total = wide(own)
            for i in range(PLANE - 1):
                total += wide(self.plane[g, half, i])
            out[g, x, y, z, half] = total.astype(out.dtype)

    def wait_sent(self, g):
        wait_blocks(self.ruler, 2 * (RING - 1) * PLANE, self.send_sem.at[g, 0])
        wait_blocks(self.ruler, 2 * (PLANE - 1), self.send_sem.at[g, 1])


def kernel(
    n_seq,
    n_dp,
    siblings,
    k_ref,
    v_ref,
    s_ref,
    q_hbm,
    do_hbm,
    dq_hbm,
    out_ref,
    q_all,
    do_all,
    dq_all,
    kv,
    kv_now,
    k_rows,
    v_rows,
    key_acc,
    value_acc,
    listed_grads,
    placing,
    part,
    line_a,
    line_b,
    sum_a,
    sum_b,
    plane,
    halves,
    hidden,
    hidden_t,
    product,
    shares,
    ruler,
    load_sem,
    store_sem,
    spread_send,
    spread_recv,
    reduce_send,
    reduce_recv,
    again_send,
    again_recv,
    share_send,
    share_recv,
    summary_send,
    summary_recv,
):
    me, me_dp = lax.axis_index("seq"), lax.axis_index("dp")
    x, y, z = place()
    groups, own, tokens, q_block = q_all.shape
    heads = q_block // HEAD
    span = k_ref.shape[1]
    listed = siblings.shape[2]
    reach = listed * span
    rows = n_seq * own * span
    scale = 1.0 / math.sqrt(HEAD)
    power = scale * math.log2(math.e)

    barrier = pltpu.get_barrier_semaphore()
    signal_peers(barrier, "seq", me, n_seq)
    signal_peers(barrier, "dp", me_dp, n_dp)
    loads = []
    for g in range(groups):
        cols = pl.ds(g * q_block, q_block)
        for c in range(own):
            loads.append(pltpu.make_async_copy(q_hbm.at[0, c, :, cols], q_all.at[g, c], load_sem.at[0, g, c]))
            loads.append(pltpu.make_async_copy(do_hbm.at[0, c, :, cols], do_all.at[g, c], load_sem.at[1, g, c]))
    for load in loads:
        load.start()
    for g in range(groups):
        cols = slice(g * HEAD, (g + 1) * HEAD)
        kv[g, x, y, z, :, :, :HEAD] = k_ref[:, :, cols]
        kv[g, x, y, z, :, :, HEAD:] = v_ref[:, :, cols]
    pl.semaphore_wait(barrier, n_seq + n_dp - 2)

    first = Spread(kv, ruler, spread_send, spread_recv)
    again = Spread(halves, ruler, again_send, again_recv)
    summing = Reduce(part, line_a, line_b, sum_a, sum_b, plane, ruler, reduce_send, reduce_recv)

    def over_groups(step):
        def one(g, carry):
            step(g)
            return carry

        lax.fori_loop(0, groups, one, 0)

    over_groups(first.start_plane)

    lane = lax.broadcasted_iota(jnp.int32, (1, own * reach), 1)
    target = lax.rem(lane, span)
    for c in range(own):
        for j in range(listed):
            here = lane // span == c * listed + j
            target += jnp.where(here, siblings[0, c, j] * span, 0)
    row = lax.broadcasted_iota(jnp.int32, (rows, own * reach), 0)
    placing[...] = jnp.where(row == target, 1.0, 0.0).astype(jnp.bfloat16)

    def line(g):
        first.wait_plane(g)
        first.start_line(g)

    over_groups(line)

    hidden[me] = s_ref[me]

    def push_summary(i, carry):
        peer = lax.rem(me + i, n_seq)
        remote(
            s_ref.at[peer], hidden.at[me], {"seq": peer}, summary_send.at[0], summary_recv.at[0]
        ).start()
        return carry

    lax.fori_loop(1, n_seq, push_summary, 0)
    for load in loads:
        load.wait()

    def attend(g, c, r):
        cols = slice(r * HEAD, (r + 1) * HEAD)
        keys, values = k_rows[...], v_rows[...]
        q, do = q_all[g, c, :, cols], do_all[g, c, :, cols]
        across = (((1,), (1,)), ((), ()))
        scores = lax.dot_general(keys, q, across, preferred_element_type=jnp.float32)
        prob_grad = lax.dot_general(values, do, across, preferred_element_type=jnp.float32)
        largest = jnp.max(scores, axis=0, keepdims=True)
        exponent = jnp.exp2((scores - largest) * power)
        prob = exponent * (1.0 / jnp.sum(exponent, axis=0, keepdims=True))
        prob_half = prob.astype(jnp.bfloat16)
        delta = jnp.sum(prob * prob_grad, axis=0, keepdims=True)
        score_half = (prob * (prob_grad - delta)).astype(jnp.bfloat16)
        value_term = jnp.dot(prob_half, do, preferred_element_type=jnp.float32)
        key_term = jnp.dot(score_half, q, preferred_element_type=jnp.float32)
        dq_t = jnp.dot(keys.T, score_half, preferred_element_type=jnp.float32)
        dq_all[g, c, :, cols] = (dq_t * scale).astype(jnp.bfloat16).T
        if r == 0:
            key_acc[...] = key_term
            value_acc[...] = value_term
        else:
            key_acc[...] += key_term
            value_acc[...] += value_term

    def begin(c):
        for j in range(listed):
            block = kv_now[siblings[0, c, j]]
            k_rows[j * span : (j + 1) * span, :] = block[:, :HEAD]
            v_rows[j * span : (j + 1) * span, :] = block[:, HEAD:]

    def end(g, c):
        listed_grads[c * reach : (c + 1) * reach, :HEAD] = (key_acc[...] * scale).astype(jnp.bfloat16)
        listed_grads[c * reach : (c + 1) * reach, HEAD:] = value_acc[...].astype(jnp.bfloat16)
        cols = pl.ds(pl.multiple_of(g * q_block, HEAD), q_block)
        pltpu.make_async_copy(dq_all.at[g, c], dq_hbm.at[0, c, :, cols], store_sem.at[g, c]).start()

    def again_plane(g):
        summing.finish(g, halves)
        again.start_plane(g)

    def again_line(g):
        again.wait_plane(g)
        again.start_line(g)

    def weigh(g):
        again.wait_line(g)
        grads = halves[g].reshape(rows, 2 * HEAD)
        got = jnp.dot(hidden_t[...], grads, preferred_element_type=jnp.float32)
        product[g] = got.reshape(product.shape[1:])
        shares[g, me_dp] = product[g, me_dp]
        for i in range(1, n_dp):
            peer = lax.rem(me_dp + i, n_dp)
            remote(
                product.at[g, peer],
                shares.at[g, me_dp],
                {"dp": peer},
                share_send.at[g],
                share_recv.at[g],
            ).start()

    def turn(it, carry):
        working = it < groups

        def slot(step, lag):
            g = it - lag

            @pl.when(jnp.logical_and(g >= 0, g < groups))
            def _():
                step(g)

        def run(c, chosen):
            @pl.when(working)
            def _():
                if 0 in chosen:
                    if c == 0:
                        first.wait_line(it)
                        kv_now[...] = kv[it].reshape(kv_now.shape)
                    begin(c)
                for r in chosen:
                    attend(it, c, r)
                if heads - 1 in chosen:
                    end(it, c)

        run(0, range(0, 2 * heads // 5))
        slot(again_line, 3)
        run(0, range(2 * heads // 5, heads))
        slot(again_plane, 2)
        run(1, range(0, 3 * heads // 5))
        slot(summing.line_to_plane, 1)
        run(1, range(3 * heads // 5, heads))

        @pl.when(working)
        def _():
            got = jnp.dot(placing[...], listed_grads[...], preferred_element_type=jnp.float32)
            part[it] = got.astype(jnp.bfloat16).reshape(part.shape[1:])
            summing.start_line(it)

        @pl.when(it == 2)
        def _():
            wait_blocks(hidden, n_seq - 1, summary_recv.at[0])
            hidden_t[...] = hidden[...].reshape(rows, hidden.shape[2]).T

        slot(weigh, 3)
        return carry

    lax.fori_loop(0, groups + 3, turn, 0)
    half = out_ref.shape[1] // 2
    for g in range(groups):
        wait_blocks(shares.at[g], n_dp - 1, share_recv.at[g])
        result = shares[g, 0]
        for d in range(1, n_dp):
            result = result + shares[g, d]
        out_ref[:, g * HEAD : (g + 1) * HEAD] = result[:, :HEAD]
        out_ref[:, half + g * HEAD : half + (g + 1) * HEAD] = result[:, HEAD:]

    def drain(g):
        first.wait_sent(g)
        again.wait_sent(g)
        summing.wait_sent(g)
        wait_blocks(shares.at[g], n_dp - 1, share_send.at[g])
        for c in range(own):
            pltpu.make_async_copy(
                dq_all.at[g, c], dq_hbm.at[0, c, :, pl.ds(0, q_block)], store_sem.at[g, c]
            ).wait()

    over_groups(drain)
    wait_blocks(hidden, n_seq - 1, summary_send.at[0])


def per_device(n_dp, n_seq, siblings, queries, grad_out, keys_in, input_values, summary):
    _, own, tokens, q_width = queries.shape
    span, kv_width = keys_in.shape[2], keys_in.shape[3]
    listed = siblings.shape[2]
    groups = kv_width // HEAD
    q_block = q_width // groups
    rows = own * span
    everyone = n_seq * rows
    block = summary.shape[3] // (n_dp * n_seq)
    any_space = pl.BlockSpec(memory_space=pl.ANY)
    vmem = pl.BlockSpec(memory_space=pltpu.VMEM)
    smem = pl.BlockSpec(memory_space=pltpu.SMEM)
    pieces = (
        summary.reshape(rows, n_dp, n_seq, block)
        .transpose(2, 0, 1, 3)
        .reshape(n_seq, rows, n_dp * block)
    )
    half = jnp.bfloat16
    tile = (span, 2 * HEAD)
    whole = pltpu.VMEM((groups, RING, 2, RING, own, *tile), half)
    tokens_all = pltpu.VMEM((groups, own, tokens, q_block), half)
    shares = pltpu.VMEM((groups, n_dp, block, 2 * HEAD), jnp.float32)
    pairs = pltpu.SemaphoreType.DMA((groups, 2))
    return pl.pallas_call(
        functools.partial(kernel, n_seq, n_dp),
        out_shape=(
            jax.ShapeDtypeStruct(queries.shape, half),
            jax.ShapeDtypeStruct((block, 2 * kv_width), jnp.float32),
        ),
        in_specs=[smem, vmem, vmem, vmem, any_space, any_space],
        out_specs=(any_space, vmem),
        scratch_shapes=[
            tokens_all,
            tokens_all,
            tokens_all,
            whole,
            pltpu.VMEM((n_seq * own, *tile), half),
            pltpu.VMEM((listed * span, HEAD), half),
            pltpu.VMEM((listed * span, HEAD), half),
            pltpu.VMEM((listed * span, HEAD), jnp.float32),
            pltpu.VMEM((listed * span, HEAD), jnp.float32),
            pltpu.VMEM((own * listed * span, 2 * HEAD), half),
            pltpu.VMEM((everyone, own * listed * span), half),
            whole,
            pltpu.VMEM((groups, RING - 1, 2, RING, *tile), half),
            pltpu.VMEM((groups, RING - 1, RING, 2, *tile), half),
            pltpu.VMEM((groups, 2, RING, *tile), half),
            pltpu.VMEM((groups, RING, 2, *tile), half),
            pltpu.VMEM((groups, 2, PLANE - 1, *tile), half),
            whole,
            pltpu.VMEM((n_seq, rows, n_dp * block), half),
            pltpu.VMEM((n_dp * block, everyone), half),
            shares,
            shares,
            pltpu.VMEM((2 * (RING - 1) * PLANE, *tile), half),
            pltpu.SemaphoreType.DMA((2, groups, own)),
            pltpu.SemaphoreType.DMA((groups, own)),
            *[pairs] * 6,
            pltpu.SemaphoreType.DMA((groups,)),
            pltpu.SemaphoreType.DMA((groups,)),
            pltpu.SemaphoreType.DMA((1,)),
            pltpu.SemaphoreType.DMA((1,)),
        ],
        compiler_params=pltpu.CompilerParams(
            collective_id=0, has_side_effects=True, vmem_limit_bytes=LIMIT
        ),
    )(siblings, keys_in[0], input_values[0], pieces, queries, grad_out)


def solution(mesh):
    placed = (
        P("dp", "seq", None),
        P("dp", "seq", None, None),
        P("dp", "seq", None, None),
        P("dp", "seq", None, None),
        P("dp", "seq", None, None),
        P("dp", "seq", None, None),
    )
    return jax.shard_map(
        functools.partial(per_device, mesh.shape["dp"], mesh.shape["seq"]),
        mesh=mesh,
        in_specs=placed,
        out_specs=(P("dp", "seq", None, None), P(("dp", "seq"), None)),
        check_vma=False,
    )
```

```python
import functools
import math

import jax
import jax.numpy as jnp
from jax import lax
from jax.experimental import pallas as pl
from jax.experimental.pallas import tpu as pltpu
from jax.sharding import PartitionSpec as P

HEAD = 128
MESH = pl.DeviceIdType.MESH
LIMIT = 56 * 1024 * 1024
RING = 4
PART = 256
PLANE = 2 * RING


def signal_peers(barrier, axis, me, count):
    def one(i, carry):
        pl.semaphore_signal(
            barrier,
            inc=1,
            device_id={axis: lax.rem(me + i, count)},
            device_id_type=MESH,
        )
        return carry

    lax.fori_loop(1, count, one, 0)


def wait_blocks(ref, count, sem):
    part = ref.at[pl.ds(0, count)]
    pltpu.make_async_copy(part, part, sem).wait()


def wide(value):
    return value.astype(jnp.float32)


def ring(at, shift):
    return lax.rem(at + shift, RING)


def place():
    me = lax.axis_index("seq")
    return me // PLANE, lax.rem(me // RING, 2), lax.rem(me, RING)


def peer_id(x, y, z):
    return {"seq": x * PLANE + y * RING + z}


def remote(src, dst, peer, send_sem, recv_sem):
    return pltpu.make_async_remote_copy(
        src_ref=src,
        dst_ref=dst,
        send_sem=send_sem,
        recv_sem=recv_sem,
        device_id=peer,
        device_id_type=MESH,
    )


def plane_shifts():
    return [(i // RING, i % RING) for i in range(1, PLANE)]


class Spread:
    def __init__(self, buf, ruler, send_sem, recv_sem):
        self.buf, self.ruler = buf, ruler
        self.send_sem, self.recv_sem = send_sem, recv_sem

    def start_plane(self, g):
        x, y, z = place()
        for dy, shift in plane_shifts():
            other = lax.rem(y + dy, 2)
            for half, peer in (
                (0, peer_id(x, other, ring(z, shift))),
                (1, peer_id(ring(x, shift), other, z)),
            ):
                block = self.buf.at[g, x, y, z, half]
                remote(block, block, peer, self.send_sem.at[g, 0], self.recv_sem.at[g, 0]).start()

    def wait_plane(self, g):
        wait_blocks(self.ruler, 2 * (PLANE - 1), self.recv_sem.at[g, 0])

    def start_line(self, g):
        x, y, z = place()
        for shift in (1, 3, 2):
            first = self.buf.at[g, x, :, :, 0]
            second = self.buf.at[g, :, :, z, 1]
            sems = (self.send_sem.at[g, 1], self.recv_sem.at[g, 1])
            remote(first, first, peer_id(ring(x, shift), y, z), *sems).start()
            remote(second, second, peer_id(x, y, ring(z, shift)), *sems).start()

    def wait_line(self, g):
        wait_blocks(self.ruler, 2 * (RING - 1) * PLANE, self.recv_sem.at[g, 1])

    def wait_sent(self, g):
        wait_blocks(self.ruler, 2 * (PLANE - 1), self.send_sem.at[g, 0])
        wait_blocks(self.ruler, 2 * (RING - 1) * PLANE, self.send_sem.at[g, 1])


class Reduce:
    def __init__(self, part, line_a, line_b, sum_a, sum_b, plane, ruler, send_sem, recv_sem):
        self.part, self.ruler = part, ruler
        self.line_a, self.line_b = line_a, line_b
        self.sum_a, self.sum_b, self.plane = sum_a, sum_b, plane
        self.send_sem, self.recv_sem = send_sem, recv_sem

    def start_line(self, g):
        x, y, z = place()
        sems = (self.send_sem.at[g, 0], self.recv_sem.at[g, 0])
        for shift in (1, 3, 2):
            xs, zs = ring(x, shift), ring(z, shift)
            slot = shift - 1
            remote(
                self.part.at[g, xs, :, :, 0], self.line_a.at[g, slot], peer_id(xs, y, z), *sems
            ).start()
            remote(
                self.part.at[g, :, :, zs, 1], self.line_b.at[g, slot], peer_id(x, y, zs), *sems
            ).start()

    def line_to_plane(self, g):
        x, y, z = place()
        wait_blocks(self.ruler, 2 * (RING - 1) * PLANE, self.recv_sem.at[g, 0])
        total_a = wide(self.part[g, x, :, :, 0])
        total_b = wide(self.part[g, :, :, z, 1])
        for slot in range(RING - 1):
            total_a += wide(self.line_a[g, slot])
            total_b += wide(self.line_b[g, slot])
        self.sum_a[g] = total_a.astype(jnp.bfloat16)
        self.sum_b[g] = total_b.astype(jnp.bfloat16)
        sems = (self.send_sem.at[g, 1], self.recv_sem.at[g, 1])
        for i, (dy, shift) in enumerate(plane_shifts()):
            other, xs, zs = lax.rem(y + dy, 2), ring(x, shift), ring(z, shift)
            remote(
                self.sum_a.at[g, other, zs], self.plane.at[g, 0, i], peer_id(x, other, zs), *sems
            ).start()
            remote(
                self.sum_b.at[g, xs, other], self.plane.at[g, 1, i], peer_id(xs, other, z), *sems
            ).start()

    def finish(self, g, out):
        x, y, z = place()
        wait_blocks(self.ruler, 2 * (PLANE - 1), self.recv_sem.at[g, 1])
        for half, own in ((0, self.sum_a[g, y, z]), (1, self.sum_b[g, x, y])):
            total = wide(own)
            for i in range(PLANE - 1):
                total += wide(self.plane[g, half, i])
            out[g, x, y, z, half] = total.astype(out.dtype)

    def wait_sent(self, g):
        wait_blocks(self.ruler, 2 * (RING - 1) * PLANE, self.send_sem.at[g, 0])
        wait_blocks(self.ruler, 2 * (PLANE - 1), self.send_sem.at[g, 1])


def kernel(
    n_seq,
    n_dp,
    siblings,
    k_ref,
    v_ref,
    s_ref,
    q_hbm,
    do_hbm,
    dq_hbm,
    out_ref,
    q_all,
    do_all,
    dq_all,
    kv,
    kv_now,
    k_rows,
    v_rows,
    key_acc,
    value_acc,
    listed_grads,
    placing,
    part,
    line_a,
    line_b,
    sum_a,
    sum_b,
    plane,
    halves,
    pieces,
    hidden,
    hidden_t,
    product,
    shares,
    ruler,
    load_sem,
    store_sem,
    spread_send,
    spread_recv,
    reduce_send,
    reduce_recv,
    again_send,
    again_recv,
    share_send,
    share_recv,
    summary_send,
    summary_recv,
):
    me, me_dp = lax.axis_index("seq"), lax.axis_index("dp")
    x, y, z = place()
    groups, own, tokens, q_block = q_all.shape
    heads = q_block // HEAD
    span = k_ref.shape[1]
    listed = siblings.shape[2]
    reach = listed * span
    rows = n_seq * own * span
    scale = 1.0 / math.sqrt(HEAD)
    power = scale * math.log2(math.e)

    barrier = pltpu.get_barrier_semaphore()
    signal_peers(barrier, "seq", me, n_seq)
    signal_peers(barrier, "dp", me_dp, n_dp)
    loads = []
    for g in range(groups):
        cols = pl.ds(g * q_block, q_block)
        for c in range(own):
            loads.append(pltpu.make_async_copy(q_hbm.at[0, c, :, cols], q_all.at[g, c], load_sem.at[0, g, c]))
            loads.append(pltpu.make_async_copy(do_hbm.at[0, c, :, cols], do_all.at[g, c], load_sem.at[1, g, c]))
    for load in loads:
        load.start()
    for g in range(groups):
        cols = slice(g * HEAD, (g + 1) * HEAD)
        kv[g, x, y, z, :, :, :HEAD] = k_ref[:, :, cols]
        kv[g, x, y, z, :, :, HEAD:] = v_ref[:, :, cols]
    pl.semaphore_wait(barrier, n_seq + n_dp - 2)

    first = Spread(kv, ruler, spread_send, spread_recv)
    again = Spread(halves, ruler, again_send, again_recv)
    summing = Reduce(part, line_a, line_b, sum_a, sum_b, plane, ruler, reduce_send, reduce_recv)

    def over_groups(step):
        def one(g, carry):
            step(g)
            return carry

        lax.fori_loop(0, groups, one, 0)

    over_groups(first.start_plane)

    lane = lax.broadcasted_iota(jnp.int32, (1, own * reach), 1)
    target = lax.rem(lane, span)
    for c in range(own):
        for j in range(listed):
            here = lane // span == c * listed + j
            target += jnp.where(here, siblings[0, c, j] * span, 0)
    row = lax.broadcasted_iota(jnp.int32, (rows, own * reach), 0)
    placing[...] = jnp.where(row == target, 1.0, 0.0).astype(jnp.bfloat16)

    def line(g):
        first.wait_plane(g)
        first.start_line(g)

    over_groups(line)

    block = pieces.shape[2] // n_dp
    step = n_seq * block
    for p in range(n_seq):
        for c in range(own):
            cut = [
                s_ref[c, :, d * step + p * block : d * step + (p + 1) * block] for d in range(n_dp)
            ]
            pieces[p, c * span : (c + 1) * span, :] = jnp.concatenate(cut, axis=1)
    hidden[me] = pieces[me]

    def push_summary(i, carry):
        peer = lax.rem(me + i, n_seq)
        remote(
            pieces.at[peer], hidden.at[me], {"seq": peer}, summary_send.at[0], summary_recv.at[0]
        ).start()
        return carry

    for load in loads:
        load.wait()

    def attend(g, c):
        keys, values = k_rows[...], v_rows[...]
        keys_t = keys.T
        size = min(PART, tokens)
        parts = [(r, t) for r in range(heads) for t in range(0, tokens, size)]
        across = (((1,), (1,)), ((), ()))

        def pick(ref, r, t):
            return ref[g, c, t : t + size, r * HEAD : (r + 1) * HEAD]

        def ahead(r, t):
            return (
                lax.dot_general(
                    keys, pick(q_all, r, t), across, preferred_element_type=jnp.float32
                ),
                lax.dot_general(
                    values, pick(do_all, r, t), across, preferred_element_type=jnp.float32
                ),
            )

        def behind(r, t, prob_half, score_half):
            value_term = jnp.dot(
                prob_half, pick(do_all, r, t), preferred_element_type=jnp.float32
            )
            key_term = jnp.dot(score_half, pick(q_all, r, t), preferred_element_type=jnp.float32)
            if (r, t) == (0, 0):
                key_acc[...] = key_term
                value_acc[...] = value_term
            else:
                key_acc[...] += key_term
                value_acc[...] += value_term
            dq_t = jnp.dot(keys_t, score_half, preferred_element_type=jnp.float32)
            dq = (dq_t * scale).astype(jnp.bfloat16).T
            dq_all[g, c, t : t + size, r * HEAD : (r + 1) * HEAD] = dq

        coming, past = ahead(*parts[0]), None
        for i, at in enumerate(parts):
            scores, prob_grad = coming
            if i + 1 < len(parts):
                coming = ahead(*parts[i + 1])
            if past is not None:
                behind(*past)
            largest = jnp.max(scores, axis=0, keepdims=True)
            exponent = jnp.exp2((scores - largest) * power)
            prob = exponent * (1.0 / jnp.sum(exponent, axis=0, keepdims=True))
            delta = jnp.sum(prob * prob_grad, axis=0, keepdims=True)
            score_half = (prob * (prob_grad - delta)).astype(jnp.bfloat16)
            past = (*at, prob.astype(jnp.bfloat16), score_half)
        behind(*past)

    def begin(c):
        for j in range(listed):
            block = kv_now[siblings[0, c, j]]
            k_rows[j * span : (j + 1) * span, :] = block[:, :HEAD]
            v_rows[j * span : (j + 1) * span, :] = block[:, HEAD:]

    def end(g, c):
        listed_grads[c * reach : (c + 1) * reach, :HEAD] = (key_acc[...] * scale).astype(jnp.bfloat16)
        listed_grads[c * reach : (c + 1) * reach, HEAD:] = value_acc[...].astype(jnp.bfloat16)
        cols = pl.ds(pl.multiple_of(g * q_block, HEAD), q_block)
        pltpu.make_async_copy(dq_all.at[g, c], dq_hbm.at[0, c, :, cols], store_sem.at[g, c]).start()

    def again_plane(g):
        summing.finish(g, halves)
        again.start_plane(g)

    def again_line(g):
        again.wait_plane(g)
        again.start_line(g)

    def weigh(g):
        again.wait_line(g)
        grads = halves[g].reshape(rows, 2 * HEAD)
        got = jnp.dot(hidden_t[...], grads, preferred_element_type=jnp.float32)
        product[g] = got.reshape(product.shape[1:])
        shares[g, me_dp] = product[g, me_dp]
        for i in range(1, n_dp):
            peer = lax.rem(me_dp + i, n_dp)
            remote(
                product.at[g, peer],
                shares.at[g, me_dp],
                {"dp": peer},
                share_send.at[g],
                share_recv.at[g],
            ).start()

    def turn(it, carry):
        first.wait_line(it)
        kv_now[...] = kv[it].reshape(kv_now.shape)
        for c in range(own):
            if c == own - 1:

                @pl.when(it >= 2)
                def _():
                    summing.line_to_plane(it - 2)

            begin(c)
            attend(it, c)
            end(it, c)
        got = jnp.dot(placing[...], listed_grads[...], preferred_element_type=jnp.float32)
        part[it] = got.astype(jnp.bfloat16).reshape(part.shape[1:])
        summing.start_line(it)

        @pl.when(it == 0)
        def _():
            lax.fori_loop(1, n_seq, push_summary, 0)

        return carry

    lax.fori_loop(0, groups, turn, 0)
    wait_blocks(hidden, n_seq - 1, summary_recv.at[0])
    hidden_t[...] = hidden[...].reshape(rows, hidden.shape[2]).T
    for g in range(groups - 2):
        again_plane(g)
    for g in range(groups - 2, groups):
        summing.line_to_plane(g)
    for g in range(groups - 2):
        again_line(g)
    for g in range(groups - 2, groups):
        again_plane(g)
    for g in range(groups):
        if g < 2:
            again_line(groups - 2 + g)
        weigh(g)
    half = out_ref.shape[1] // 2
    for g in range(groups):
        wait_blocks(shares.at[g], n_dp - 1, share_recv.at[g])
        result = shares[g, 0]
        for d in range(1, n_dp):
            result = result + shares[g, d]
        out_ref[:, g * HEAD : (g + 1) * HEAD] = result[:, :HEAD]
        out_ref[:, half + g * HEAD : half + (g + 1) * HEAD] = result[:, HEAD:]

    def drain(g):
        first.wait_sent(g)
        again.wait_sent(g)
        summing.wait_sent(g)
        wait_blocks(shares.at[g], n_dp - 1, share_send.at[g])
        for c in range(own):
            pltpu.make_async_copy(
                dq_all.at[g, c], dq_hbm.at[0, c, :, pl.ds(0, q_block)], store_sem.at[g, c]
            ).wait()

    over_groups(drain)
    wait_blocks(hidden, n_seq - 1, summary_send.at[0])


def per_device(n_dp, n_seq, siblings, queries, grad_out, keys_in, input_values, summary):
    _, own, tokens, q_width = queries.shape
    span, kv_width = keys_in.shape[2], keys_in.shape[3]
    listed = siblings.shape[2]
    groups = kv_width // HEAD
    q_block = q_width // groups
    rows = own * span
    everyone = n_seq * rows
    block = summary.shape[3] // (n_dp * n_seq)
    any_space = pl.BlockSpec(memory_space=pl.ANY)
    vmem = pl.BlockSpec(memory_space=pltpu.VMEM)
    smem = pl.BlockSpec(memory_space=pltpu.SMEM)
    half = jnp.bfloat16
    tile = (span, 2 * HEAD)
    whole = pltpu.VMEM((groups, RING, 2, RING, own, *tile), half)
    tokens_all = pltpu.VMEM((groups, own, tokens, q_block), half)
    shares = pltpu.VMEM((groups, n_dp, block, 2 * HEAD), jnp.float32)
    pairs = pltpu.SemaphoreType.DMA((groups, 2))
    return pl.pallas_call(
        functools.partial(kernel, n_seq, n_dp),
        out_shape=(
            jax.ShapeDtypeStruct(queries.shape, half),
            jax.ShapeDtypeStruct((block, 2 * kv_width), jnp.float32),
        ),
        in_specs=[smem, vmem, vmem, vmem, any_space, any_space],
        out_specs=(any_space, vmem),
        scratch_shapes=[
            tokens_all,
            tokens_all,
            tokens_all,
            whole,
            pltpu.VMEM((n_seq * own, *tile), half),
            pltpu.VMEM((listed * span, HEAD), half),
            pltpu.VMEM((listed * span, HEAD), half),
            pltpu.VMEM((listed * span, HEAD), jnp.float32),
            pltpu.VMEM((listed * span, HEAD), jnp.float32),
            pltpu.VMEM((own * listed * span, 2 * HEAD), half),
            pltpu.VMEM((everyone, own * listed * span), half),
            whole,
            pltpu.VMEM((groups, RING - 1, 2, RING, *tile), half),
            pltpu.VMEM((groups, RING - 1, RING, 2, *tile), half),
            pltpu.VMEM((groups, 2, RING, *tile), half),
            pltpu.VMEM((groups, RING, 2, *tile), half),
            pltpu.VMEM((groups, 2, PLANE - 1, *tile), half),
            whole,
            pltpu.VMEM((n_seq, rows, n_dp * block), half),
            pltpu.VMEM((n_seq, rows, n_dp * block), half),
            pltpu.VMEM((n_dp * block, everyone), half),
            shares,
            shares,
            pltpu.VMEM((2 * (RING - 1) * PLANE, *tile), half),
            pltpu.SemaphoreType.DMA((2, groups, own)),
            pltpu.SemaphoreType.DMA((groups, own)),
            *[pairs] * 6,
            pltpu.SemaphoreType.DMA((groups,)),
            pltpu.SemaphoreType.DMA((groups,)),
            pltpu.SemaphoreType.DMA((1,)),
            pltpu.SemaphoreType.DMA((1,)),
        ],
        compiler_params=pltpu.CompilerParams(
            collective_id=0, has_side_effects=True, vmem_limit_bytes=LIMIT
        ),
    )(siblings, keys_in[0], input_values[0], summary[0], queries, grad_out)


def solution(mesh):
    placed = (
        P("dp", "seq", None),
        P("dp", "seq", None, None),
        P("dp", "seq", None, None),
        P("dp", "seq", None, None),
        P("dp", "seq", None, None),
        P("dp", "seq", None, None),
    )
    return jax.shard_map(
        functools.partial(per_device, mesh.shape["dp"], mesh.shape["seq"]),
        mesh=mesh,
        in_specs=placed,
        out_specs=(P("dp", "seq", None, None), P(("dp", "seq"), None)),
        check_vma=False,
    )
```

```python
import functools
import math

import jax
import jax.numpy as jnp
from jax import lax
from jax.experimental import pallas as pl
from jax.experimental.pallas import tpu as pltpu
from jax.sharding import PartitionSpec as P

HEAD = 128
MESH = pl.DeviceIdType.MESH
LIMIT = 56 * 1024 * 1024
RING = 4
PART = 256
PLANE = 2 * RING


def signal_peers(barrier, axis, me, count):
    def one(i, carry):
        pl.semaphore_signal(
            barrier,
            inc=1,
            device_id={axis: lax.rem(me + i, count)},
            device_id_type=MESH,
        )
        return carry

    lax.fori_loop(1, count, one, 0)


def wait_blocks(ref, count, sem):
    part = ref.at[pl.ds(0, count)]
    pltpu.make_async_copy(part, part, sem).wait()


def wide(value):
    return value.astype(jnp.float32)


def ring(at, shift):
    return lax.rem(at + shift, RING)


def place():
    me = lax.axis_index("seq")
    return me // PLANE, lax.rem(me // RING, 2), lax.rem(me, RING)


def peer_id(x, y, z):
    return {"seq": x * PLANE + y * RING + z}


def remote(src, dst, peer, send_sem, recv_sem):
    return pltpu.make_async_remote_copy(
        src_ref=src,
        dst_ref=dst,
        send_sem=send_sem,
        recv_sem=recv_sem,
        device_id=peer,
        device_id_type=MESH,
    )


def plane_shifts():
    return [(i // RING, i % RING) for i in range(1, PLANE)]


class Spread:
    def __init__(self, buf, ruler, send_sem, recv_sem):
        self.buf, self.ruler = buf, ruler
        self.send_sem, self.recv_sem = send_sem, recv_sem

    def start_plane(self, g):
        x, y, z = place()
        for dy, shift in plane_shifts():
            other = lax.rem(y + dy, 2)
            for half, peer in (
                (0, peer_id(x, other, ring(z, shift))),
                (1, peer_id(ring(x, shift), other, z)),
            ):
                block = self.buf.at[g, x, y, z, half]
                remote(block, block, peer, self.send_sem.at[g, 0], self.recv_sem.at[g, 0]).start()

    def wait_plane(self, g):
        wait_blocks(self.ruler, 2 * (PLANE - 1), self.recv_sem.at[g, 0])

    def start_line(self, g):
        x, y, z = place()
        for shift in (1, 3, 2):
            first = self.buf.at[g, x, :, :, 0]
            second = self.buf.at[g, :, :, z, 1]
            sems = (self.send_sem.at[g, 1], self.recv_sem.at[g, 1])
            remote(first, first, peer_id(ring(x, shift), y, z), *sems).start()
            remote(second, second, peer_id(x, y, ring(z, shift)), *sems).start()

    def wait_line(self, g):
        wait_blocks(self.ruler, 2 * (RING - 1) * PLANE, self.recv_sem.at[g, 1])

    def wait_sent(self, g):
        wait_blocks(self.ruler, 2 * (PLANE - 1), self.send_sem.at[g, 0])
        wait_blocks(self.ruler, 2 * (RING - 1) * PLANE, self.send_sem.at[g, 1])


class Halves:
    def __init__(self, own, buf, ruler, send_sem, recv_sem):
        self.own, self.buf, self.ruler = own, buf, ruler
        self.send_sem, self.recv_sem = send_sem, recv_sem

    def start_plane(self, g):
        x, y, z = place()
        self.buf[g, x, y, z] = self.own[g, y]
        sems = (self.send_sem.at[g, 0], self.recv_sem.at[g, 0])
        for dy, shift in plane_shifts():
            other = lax.rem(y + dy, 2)
            for half, peer in (
                (0, peer_id(x, other, ring(z, shift))),
                (1, peer_id(ring(x, shift), other, z)),
            ):
                remote(
                    self.own.at[g, other, half], self.buf.at[g, x, y, z, half], peer, *sems
                ).start()

    def start_line(self, g):
        x, y, z = place()
        wait_blocks(self.ruler, PLANE - 1, self.recv_sem.at[g, 0])
        sems = (self.send_sem.at[g, 1], self.recv_sem.at[g, 1])
        for shift in (1, 3, 2):
            first = self.buf.at[g, x, :, :, 0]
            second = self.buf.at[g, :, :, z, 1]
            remote(first, first, peer_id(ring(x, shift), y, z), *sems).start()
            remote(second, second, peer_id(x, y, ring(z, shift)), *sems).start()

    def wait_line(self, g):
        wait_blocks(self.ruler, (RING - 1) * PLANE, self.recv_sem.at[g, 1])

    def wait_sent(self, g):
        wait_blocks(self.ruler, PLANE - 1, self.send_sem.at[g, 0])
        wait_blocks(self.ruler, (RING - 1) * PLANE, self.send_sem.at[g, 1])


class Reduce:
    def __init__(self, part, line_a, line_b, sum_a, sum_b, plane, ruler, send_sem, recv_sem):
        self.part, self.ruler = part, ruler
        self.line_a, self.line_b = line_a, line_b
        self.sum_a, self.sum_b, self.plane = sum_a, sum_b, plane
        self.send_sem, self.recv_sem = send_sem, recv_sem

    def start_line(self, g):
        x, y, z = place()
        sems = (self.send_sem.at[g, 0], self.recv_sem.at[g, 0])
        for shift in (1, 3, 2):
            xs, zs = ring(x, shift), ring(z, shift)
            slot = shift - 1
            remote(
                self.part.at[g, xs, :, :, 0], self.line_a.at[g, slot], peer_id(xs, y, z), *sems
            ).start()
            remote(
                self.part.at[g, :, :, zs, 1], self.line_b.at[g, slot], peer_id(x, y, zs), *sems
            ).start()

    def line_to_plane(self, g):
        x, y, z = place()
        wait_blocks(self.ruler, 2 * (RING - 1) * PLANE, self.recv_sem.at[g, 0])
        total_a = wide(self.part[g, x, :, :, 0])
        total_b = wide(self.part[g, :, :, z, 1])
        for slot in range(RING - 1):
            total_a += wide(self.line_a[g, slot])
            total_b += wide(self.line_b[g, slot])
        self.sum_a[g] = total_a.astype(jnp.bfloat16)
        self.sum_b[g] = total_b.astype(jnp.bfloat16)
        sems = (self.send_sem.at[g, 1], self.recv_sem.at[g, 1])
        for i, (dy, shift) in enumerate(plane_shifts()):
            other, xs, zs = lax.rem(y + dy, 2), ring(x, shift), ring(z, shift)
            remote(
                self.sum_a.at[g, other, zs], self.plane.at[g, 0, i], peer_id(x, other, zs), *sems
            ).start()
            remote(
                self.sum_b.at[g, xs, other], self.plane.at[g, 1, i], peer_id(xs, other, z), *sems
            ).start()

    def finish(self, g, out):
        x, y, z = place()
        wait_blocks(self.ruler, 2 * (PLANE - 1), self.recv_sem.at[g, 1])
        for half, own in ((0, self.sum_a[g, y, z]), (1, self.sum_b[g, x, y])):
            total = wide(own)
            for i in range(PLANE - 1):
                total += wide(self.plane[g, half, i])
            total = total.astype(jnp.bfloat16)
            for which in range(2):
                out.own[g, which, half] = total[:, which * HEAD : (which + 1) * HEAD]

    def wait_sent(self, g):
        wait_blocks(self.ruler, 2 * (RING - 1) * PLANE, self.send_sem.at[g, 0])
        wait_blocks(self.ruler, 2 * (PLANE - 1), self.send_sem.at[g, 1])


def kernel(
    n_seq,
    n_dp,
    siblings,
    k_ref,
    v_ref,
    s_ref,
    q_hbm,
    do_hbm,
    dq_hbm,
    out_ref,
    q_all,
    do_all,
    dq_all,
    kv,
    kv_now,
    k_rows,
    v_rows,
    key_acc,
    value_acc,
    listed_grads,
    placing,
    part,
    line_a,
    line_b,
    sum_a,
    sum_b,
    plane,
    sum_own,
    sums,
    pieces,
    hidden,
    hidden_t,
    product,
    shares,
    ruler,
    load_sem,
    store_sem,
    spread_send,
    spread_recv,
    reduce_send,
    reduce_recv,
    again_send,
    again_recv,
    share_send,
    share_recv,
    summary_send,
    summary_recv,
):
    me, me_dp = lax.axis_index("seq"), lax.axis_index("dp")
    x, y, z = place()
    groups, own, tokens, q_block = q_all.shape
    heads = q_block // HEAD
    span = k_ref.shape[1]
    listed = siblings.shape[2]
    reach = listed * span
    rows = n_seq * own * span
    scale = 1.0 / math.sqrt(HEAD)
    power = scale * math.log2(math.e)

    barrier = pltpu.get_barrier_semaphore()
    signal_peers(barrier, "seq", me, n_seq)
    for i in range(1, n_dp):
        for across_y in range(2):
            pl.semaphore_signal(
                barrier,
                inc=1,
                device_id={"dp": lax.rem(me_dp + i, n_dp), **peer_id(x, across_y, z)},
                device_id_type=MESH,
            )
    loads = []
    for g in range(groups):
        cols = pl.ds(g * q_block, q_block)
        for c in range(own):
            loads.append(pltpu.make_async_copy(q_hbm.at[0, c, :, cols], q_all.at[g, c], load_sem.at[0, g, c]))
            loads.append(pltpu.make_async_copy(do_hbm.at[0, c, :, cols], do_all.at[g, c], load_sem.at[1, g, c]))
    for load in loads:
        load.start()
    for g in range(groups):
        cols = slice(g * HEAD, (g + 1) * HEAD)
        kv[g, x, y, z, :, :, :HEAD] = k_ref[:, :, cols]
        kv[g, x, y, z, :, :, HEAD:] = v_ref[:, :, cols]
    pl.semaphore_wait(barrier, n_seq - 1 + 2 * (n_dp - 1))

    first = Spread(kv, ruler, spread_send, spread_recv)
    again = Halves(sum_own, sums, ruler, again_send, again_recv)
    summing = Reduce(part, line_a, line_b, sum_a, sum_b, plane, ruler, reduce_send, reduce_recv)

    def over_groups(step):
        def one(g, carry):
            step(g)
            return carry

        lax.fori_loop(0, groups, one, 0)

    over_groups(first.start_plane)

    lane = lax.broadcasted_iota(jnp.int32, (1, own * reach), 1)
    target = lax.rem(lane, span)
    for c in range(own):
        for j in range(listed):
            here = lane // span == c * listed + j
            target += jnp.where(here, siblings[0, c, j] * span, 0)
    row = lax.broadcasted_iota(jnp.int32, (rows, own * reach), 0)
    placing[...] = jnp.where(row == target, 1.0, 0.0).astype(jnp.bfloat16)

    def line(g):
        first.wait_plane(g)
        first.start_line(g)

    over_groups(line)

    taken = pieces.shape[3] // own
    block = taken // (2 * n_dp)
    step = n_seq * block
    for xs in range(RING):
        for zs in range(RING):
            starts = [
                d * step + (xs * PLANE + ys * RING + zs) * block
                for d in range(n_dp)
                for ys in range(2)
            ]
            cut = [s_ref[c, :, at : at + block] for c in range(own) for at in starts]
            pieces[xs, zs] = jnp.concatenate(cut, axis=1)
    hidden[me] = pieces[x, z]

    def push_summary(i, carry):
        peer = lax.rem(me + i, n_seq)
        remote(
            pieces.at[peer // PLANE, lax.rem(peer, RING)],
            hidden.at[me],
            {"seq": peer},
            summary_send.at[0],
            summary_recv.at[0],
        ).start()
        return carry

    for load in loads:
        load.wait()

    def attend(g, c):
        keys, values = k_rows[...], v_rows[...]
        keys_t = keys.T
        size = min(PART, tokens)
        parts = [(r, t) for r in range(heads) for t in range(0, tokens, size)]
        across = (((1,), (1,)), ((), ()))

        def pick(ref, r, t):
            return ref[g, c, t : t + size, r * HEAD : (r + 1) * HEAD]

        def ahead(r, t):
            return (
                lax.dot_general(
                    keys, pick(q_all, r, t), across, preferred_element_type=jnp.float32
                ),
                lax.dot_general(
                    values, pick(do_all, r, t), across, preferred_element_type=jnp.float32
                ),
            )

        def behind(r, t, prob_half, score_half):
            value_term = jnp.dot(
                prob_half, pick(do_all, r, t), preferred_element_type=jnp.float32
            )
            key_term = jnp.dot(score_half, pick(q_all, r, t), preferred_element_type=jnp.float32)
            if (r, t) == (0, 0):
                key_acc[...] = key_term
                value_acc[...] = value_term
            else:
                key_acc[...] += key_term
                value_acc[...] += value_term
            dq_t = jnp.dot(keys_t, score_half, preferred_element_type=jnp.float32)
            dq = (dq_t * scale).astype(jnp.bfloat16).T
            dq_all[g, c, t : t + size, r * HEAD : (r + 1) * HEAD] = dq

        coming, past = ahead(*parts[0]), None
        for i, at in enumerate(parts):
            scores, prob_grad = coming
            if i + 1 < len(parts):
                coming = ahead(*parts[i + 1])
            if past is not None:
                behind(*past)
            largest = jnp.max(scores, axis=0, keepdims=True)
            exponent = jnp.exp2((scores - largest) * power)
            prob = exponent * (1.0 / jnp.sum(exponent, axis=0, keepdims=True))
            delta = jnp.sum(prob * prob_grad, axis=0, keepdims=True)
            score_half = (prob * (prob_grad - delta)).astype(jnp.bfloat16)
            past = (*at, prob.astype(jnp.bfloat16), score_half)
        behind(*past)

    def begin(c):
        for j in range(listed):
            block = kv_now[siblings[0, c, j]]
            k_rows[j * span : (j + 1) * span, :] = block[:, :HEAD]
            v_rows[j * span : (j + 1) * span, :] = block[:, HEAD:]

    def end(g, c):
        listed_grads[c * reach : (c + 1) * reach, :HEAD] = (key_acc[...] * scale).astype(jnp.bfloat16)
        listed_grads[c * reach : (c + 1) * reach, HEAD:] = value_acc[...].astype(jnp.bfloat16)
        cols = pl.ds(pl.multiple_of(g * q_block, HEAD), q_block)
        pltpu.make_async_copy(dq_all.at[g, c], dq_hbm.at[0, c, :, cols], store_sem.at[g, c]).start()

    def again_plane(g):
        summing.finish(g, again)
        again.start_plane(g)

    def again_line(g):
        again.start_line(g)

    def weigh(g):
        again.wait_line(g)
        got = 0.0
        for c in range(own):
            grads = sums[g, :, :, :, c].reshape(rows // own, HEAD)
            got += jnp.dot(hidden_t[c], grads, preferred_element_type=jnp.float32)
        product[g] = got.reshape(product.shape[1:])
        mine = me_dp * 2 + y
        shares[g, mine] = product[g, mine]
        for i in range(1, 2 * n_dp):
            d, ys = lax.rem(me_dp + i // 2, n_dp), lax.rem(y + i % 2, 2)
            remote(
                product.at[g, d * 2 + ys],
                shares.at[g, mine],
                {"dp": d, **peer_id(x, ys, z)},
                share_send.at[g],
                share_recv.at[g],
            ).start()

    def turn(it, carry):
        first.wait_line(it)
        kv_now[...] = kv[it].reshape(kv_now.shape)
        for c in range(own):
            if c == own - 1:

                @pl.when(it >= 2)
                def _():
                    summing.line_to_plane(it - 2)

            begin(c)
            attend(it, c)
            end(it, c)
        got = jnp.dot(placing[...], listed_grads[...], preferred_element_type=jnp.float32)
        part[it] = got.astype(jnp.bfloat16).reshape(part.shape[1:])
        summing.start_line(it)

        @pl.when(it == 1)
        def _():
            lax.fori_loop(1, n_seq, push_summary, 0)

        return carry

    lax.fori_loop(0, groups, turn, 0)
    wait_blocks(hidden, n_seq - 1, summary_recv.at[0])
    for c in range(own):
        columns = hidden[:, :, c * taken : (c + 1) * taken]
        hidden_t[c] = columns.reshape(rows // own, taken).T
    for g in range(groups - 2):
        again_plane(g)
    for g in range(groups - 2, groups):
        summing.line_to_plane(g)
    for g in range(groups - 2):
        again_line(g)
    for g in range(groups - 2, groups):
        again_plane(g)
    for g in range(groups):
        if g < 2:
            again_line(groups - 2 + g)
        weigh(g)
    half = out_ref.shape[1] // 2
    for g in range(groups):
        wait_blocks(shares.at[g], 2 * n_dp - 1, share_recv.at[g])
        for ys in range(2):
            result = shares[g, ys]
            for d in range(1, n_dp):
                result = result + shares[g, 2 * d + ys]
            out_ref[:, ys * half + g * HEAD : ys * half + (g + 1) * HEAD] = result

    def drain(g):
        first.wait_sent(g)
        again.wait_sent(g)
        summing.wait_sent(g)
        wait_blocks(shares.at[g], 2 * n_dp - 1, share_send.at[g])
        for c in range(own):
            pltpu.make_async_copy(
                dq_all.at[g, c], dq_hbm.at[0, c, :, pl.ds(0, q_block)], store_sem.at[g, c]
            ).wait()

    over_groups(drain)
    wait_blocks(hidden, n_seq - 1, summary_send.at[0])


def per_device(n_dp, n_seq, siblings, queries, grad_out, keys_in, input_values, summary):
    _, own, tokens, q_width = queries.shape
    span, kv_width = keys_in.shape[2], keys_in.shape[3]
    listed = siblings.shape[2]
    groups = kv_width // HEAD
    q_block = q_width // groups
    rows = own * span
    everyone = n_seq * rows
    block = summary.shape[3] // (n_dp * n_seq)
    any_space = pl.BlockSpec(memory_space=pl.ANY)
    vmem = pl.BlockSpec(memory_space=pltpu.VMEM)
    smem = pl.BlockSpec(memory_space=pltpu.SMEM)
    half = jnp.bfloat16
    tile, thin = (span, 2 * HEAD), (span, HEAD)
    taken = 2 * n_dp * block
    whole = pltpu.VMEM((groups, RING, 2, RING, own, *tile), half)
    tokens_all = pltpu.VMEM((groups, own, tokens, q_block), half)
    shares = pltpu.VMEM((groups, 2 * n_dp, block, HEAD), jnp.float32)
    pairs = pltpu.SemaphoreType.DMA((groups, 2))
    return pl.pallas_call(
        functools.partial(kernel, n_seq, n_dp),
        out_shape=(
            jax.ShapeDtypeStruct(queries.shape, half),
            jax.ShapeDtypeStruct((block, 2 * kv_width), jnp.float32),
        ),
        in_specs=[smem, vmem, vmem, vmem, any_space, any_space],
        out_specs=(any_space, vmem),
        scratch_shapes=[
            tokens_all,
            tokens_all,
            tokens_all,
            whole,
            pltpu.VMEM((n_seq * own, *tile), half),
            pltpu.VMEM((listed * span, HEAD), half),
            pltpu.VMEM((listed * span, HEAD), half),
            pltpu.VMEM((listed * span, HEAD), jnp.float32),
            pltpu.VMEM((listed * span, HEAD), jnp.float32),
            pltpu.VMEM((own * listed * span, 2 * HEAD), half),
            pltpu.VMEM((everyone, own * listed * span), half),
            whole,
            pltpu.VMEM((groups, RING - 1, 2, RING, *tile), half),
            pltpu.VMEM((groups, RING - 1, RING, 2, *tile), half),
            pltpu.VMEM((groups, 2, RING, *tile), half),
            pltpu.VMEM((groups, RING, 2, *tile), half),
            pltpu.VMEM((groups, 2, PLANE - 1, *tile), half),
            pltpu.VMEM((groups, 2, own, *thin), half),
            pltpu.VMEM((groups, RING, 2, RING, own, *thin), half),
            pltpu.VMEM((RING, RING, span, own * taken), half),
            pltpu.VMEM((n_seq, span, own * taken), half),
            pltpu.VMEM((own, taken, everyone // own), half),
            shares,
            shares,
            pltpu.VMEM((2 * (RING - 1) * PLANE, *tile), half),
            pltpu.SemaphoreType.DMA((2, groups, own)),
            pltpu.SemaphoreType.DMA((groups, own)),
            *[pairs] * 6,
            pltpu.SemaphoreType.DMA((groups,)),
            pltpu.SemaphoreType.DMA((groups,)),
            pltpu.SemaphoreType.DMA((1,)),
            pltpu.SemaphoreType.DMA((1,)),
        ],
        compiler_params=pltpu.CompilerParams(
            collective_id=0, has_side_effects=True, vmem_limit_bytes=LIMIT
        ),
    )(siblings, keys_in[0], input_values[0], summary[0], queries, grad_out)


def solution(mesh):
    placed = (
        P("dp", "seq", None),
        P("dp", "seq", None, None),
        P("dp", "seq", None, None),
        P("dp", "seq", None, None),
        P("dp", "seq", None, None),
        P("dp", "seq", None, None),
    )
    return jax.shard_map(
        functools.partial(per_device, mesh.shape["dp"], mesh.shape["seq"]),
        mesh=mesh,
        in_specs=placed,
        out_specs=(P("dp", "seq", None, None), P(("dp", "seq"), None)),
        check_vma=False,
    )
```

```python
import functools
import math

import jax
import jax.numpy as jnp
from jax import lax
from jax.experimental import pallas as pl
from jax.experimental.pallas import tpu as pltpu
from jax.sharding import PartitionSpec as P

HEAD = 128
MESH = pl.DeviceIdType.MESH
LIMIT = 56 * 1024 * 1024
RING = 4
PART = 256
PLANE = 2 * RING


def signal_peers(barrier, axis, me, count):
    def one(i, carry):
        pl.semaphore_signal(
            barrier,
            inc=1,
            device_id={axis: lax.rem(me + i, count)},
            device_id_type=MESH,
        )
        return carry

    lax.fori_loop(1, count, one, 0)


def wait_blocks(ref, count, sem):
    part = ref.at[pl.ds(0, count)]
    pltpu.make_async_copy(part, part, sem).wait()


def wide(value):
    return value.astype(jnp.float32)


def ring(at, shift):
    return lax.rem(at + shift, RING)


def place():
    me = lax.axis_index("seq")
    return me // PLANE, lax.rem(me // RING, 2), lax.rem(me, RING)


def peer_id(x, y, z):
    return {"seq": x * PLANE + y * RING + z}


def remote(src, dst, peer, send_sem, recv_sem):
    return pltpu.make_async_remote_copy(
        src_ref=src,
        dst_ref=dst,
        send_sem=send_sem,
        recv_sem=recv_sem,
        device_id=peer,
        device_id_type=MESH,
    )


def plane_shifts():
    return [(1, 2), (1, 1), (1, 3), (0, 2), (1, 0), (0, 1), (0, 3)]


class Spread:
    def __init__(self, buf, ruler, send_sem, recv_sem):
        self.buf, self.ruler = buf, ruler
        self.send_sem, self.recv_sem = send_sem, recv_sem

    def start_plane(self, g):
        x, y, z = place()
        for dy, shift in plane_shifts():
            other = lax.rem(y + dy, 2)
            for half, peer in (
                (0, peer_id(x, other, ring(z, shift))),
                (1, peer_id(ring(x, shift), other, z)),
            ):
                block = self.buf.at[g, x, y, z, half]
                remote(block, block, peer, self.send_sem.at[g, 0], self.recv_sem.at[g, 0]).start()

    def wait_plane(self, g):
        wait_blocks(self.ruler, 2 * (PLANE - 1), self.recv_sem.at[g, 0])

    def start_line(self, g):
        x, y, z = place()
        for shift in (2, 1, 3):
            first = self.buf.at[g, x, :, :, 0]
            second = self.buf.at[g, :, :, z, 1]
            sems = (self.send_sem.at[g, 1], self.recv_sem.at[g, 1])
            remote(first, first, peer_id(ring(x, shift), y, z), *sems).start()
            remote(second, second, peer_id(x, y, ring(z, shift)), *sems).start()

    def wait_line(self, g):
        wait_blocks(self.ruler, 2 * (RING - 1) * PLANE, self.recv_sem.at[g, 1])

    def wait_sent(self, g):
        wait_blocks(self.ruler, 2 * (PLANE - 1), self.send_sem.at[g, 0])
        wait_blocks(self.ruler, 2 * (RING - 1) * PLANE, self.send_sem.at[g, 1])


class Halves:
    def __init__(self, own, buf, ruler, send_sem, recv_sem):
        self.own, self.buf, self.ruler = own, buf, ruler
        self.send_sem, self.recv_sem = send_sem, recv_sem

    def start_plane(self, g):
        x, y, z = place()
        self.buf[g, x, y, z] = self.own[g, y]
        sems = (self.send_sem.at[g, 0], self.recv_sem.at[g, 0])
        for dy, shift in plane_shifts():
            other = lax.rem(y + dy, 2)
            for half, peer in (
                (0, peer_id(x, other, ring(z, shift))),
                (1, peer_id(ring(x, shift), other, z)),
            ):
                remote(
                    self.own.at[g, other, half], self.buf.at[g, x, y, z, half], peer, *sems
                ).start()

    def start_line(self, g):
        x, y, z = place()
        wait_blocks(self.ruler, PLANE - 1, self.recv_sem.at[g, 0])
        sems = (self.send_sem.at[g, 1], self.recv_sem.at[g, 1])
        for shift in (2, 1, 3):
            first = self.buf.at[g, x, :, :, 0]
            second = self.buf.at[g, :, :, z, 1]
            remote(first, first, peer_id(ring(x, shift), y, z), *sems).start()
            remote(second, second, peer_id(x, y, ring(z, shift)), *sems).start()

    def wait_line(self, g):
        wait_blocks(self.ruler, (RING - 1) * PLANE, self.recv_sem.at[g, 1])

    def wait_sent(self, g):
        wait_blocks(self.ruler, PLANE - 1, self.send_sem.at[g, 0])
        wait_blocks(self.ruler, (RING - 1) * PLANE, self.send_sem.at[g, 1])


class Reduce:
    def __init__(self, part, line_a, line_b, sum_a, sum_b, plane, ruler, send_sem, recv_sem):
        self.part, self.ruler = part, ruler
        self.line_a, self.line_b = line_a, line_b
        self.sum_a, self.sum_b, self.plane = sum_a, sum_b, plane
        self.send_sem, self.recv_sem = send_sem, recv_sem

    def start_line(self, g):
        x, y, z = place()
        sems = (self.send_sem.at[g, 0], self.recv_sem.at[g, 0])
        for shift in (2, 1, 3):
            xs, zs = ring(x, shift), ring(z, shift)
            slot = shift - 1
            remote(
                self.part.at[g, xs, :, :, 0], self.line_a.at[g, slot], peer_id(xs, y, z), *sems
            ).start()
            remote(
                self.part.at[g, :, :, zs, 1], self.line_b.at[g, slot], peer_id(x, y, zs), *sems
            ).start()

    def line_to_plane(self, g):
        x, y, z = place()
        wait_blocks(self.ruler, 2 * (RING - 1) * PLANE, self.recv_sem.at[g, 0])
        total_a = wide(self.part[g, x, :, :, 0])
        total_b = wide(self.part[g, :, :, z, 1])
        for slot in range(RING - 1):
            total_a += wide(self.line_a[g, slot])
            total_b += wide(self.line_b[g, slot])
        self.sum_a[g] = total_a.astype(jnp.bfloat16)
        self.sum_b[g] = total_b.astype(jnp.bfloat16)
        sems = (self.send_sem.at[g, 1], self.recv_sem.at[g, 1])
        for i, (dy, shift) in enumerate(plane_shifts()):
            other, xs, zs = lax.rem(y + dy, 2), ring(x, shift), ring(z, shift)
            remote(
                self.sum_a.at[g, other, zs], self.plane.at[g, 0, i], peer_id(x, other, zs), *sems
            ).start()
            remote(
                self.sum_b.at[g, xs, other], self.plane.at[g, 1, i], peer_id(xs, other, z), *sems
            ).start()

    def finish(self, g, out):
        x, y, z = place()
        wait_blocks(self.ruler, 2 * (PLANE - 1), self.recv_sem.at[g, 1])
        for half, own in ((0, self.sum_a[g, y, z]), (1, self.sum_b[g, x, y])):
            total = wide(own)
            for i in range(PLANE - 1):
                total += wide(self.plane[g, half, i])
            total = total.astype(jnp.bfloat16)
            for which in range(2):
                out.own[g, which, half] = total[:, which * HEAD : (which + 1) * HEAD]

    def wait_sent(self, g):
        wait_blocks(self.ruler, 2 * (RING - 1) * PLANE, self.send_sem.at[g, 0])
        wait_blocks(self.ruler, 2 * (PLANE - 1), self.send_sem.at[g, 1])


def kernel(
    n_seq,
    n_dp,
    siblings,
    k_ref,
    v_ref,
    s_ref,
    q_hbm,
    do_hbm,
    dq_hbm,
    out_ref,
    q_all,
    do_all,
    dq_all,
    kv,
    kv_now,
    k_rows,
    v_rows,
    key_acc,
    value_acc,
    listed_grads,
    placing,
    part,
    line_a,
    line_b,
    sum_a,
    sum_b,
    plane,
    sum_own,
    sums,
    pieces,
    hidden,
    hidden_t,
    product,
    shares,
    ruler,
    load_sem,
    store_sem,
    spread_send,
    spread_recv,
    reduce_send,
    reduce_recv,
    again_send,
    again_recv,
    share_send,
    share_recv,
    summary_send,
    summary_recv,
):
    me, me_dp = lax.axis_index("seq"), lax.axis_index("dp")
    x, y, z = place()
    groups, own, tokens, q_block = q_all.shape
    heads = q_block // HEAD
    span = k_ref.shape[1]
    listed = siblings.shape[2]
    reach = listed * span
    rows = n_seq * own * span
    scale = 1.0 / math.sqrt(HEAD)
    power = scale * math.log2(math.e)

    barrier = pltpu.get_barrier_semaphore()
    signal_peers(barrier, "seq", me, n_seq)
    for i in range(1, n_dp):
        for across_y in range(2):
            pl.semaphore_signal(
                barrier,
                inc=1,
                device_id={"dp": lax.rem(me_dp + i, n_dp), **peer_id(x, across_y, z)},
                device_id_type=MESH,
            )
    loads = []
    for g in range(groups):
        cols = pl.ds(g * q_block, q_block)
        for c in range(own):
            loads.append(pltpu.make_async_copy(q_hbm.at[0, c, :, cols], q_all.at[g, c], load_sem.at[0, g, c]))
            loads.append(pltpu.make_async_copy(do_hbm.at[0, c, :, cols], do_all.at[g, c], load_sem.at[1, g, c]))
    for load in loads:
        load.start()
    for g in range(groups):
        cols = slice(g * HEAD, (g + 1) * HEAD)
        kv[g, x, y, z, :, :, :HEAD] = k_ref[:, :, cols]
        kv[g, x, y, z, :, :, HEAD:] = v_ref[:, :, cols]
    pl.semaphore_wait(barrier, n_seq - 1 + 2 * (n_dp - 1))

    first = Spread(kv, ruler, spread_send, spread_recv)
    again = Halves(sum_own, sums, ruler, again_send, again_recv)
    summing = Reduce(part, line_a, line_b, sum_a, sum_b, plane, ruler, reduce_send, reduce_recv)

    def over_groups(step):
        def one(g, carry):
            step(g)
            return carry

        lax.fori_loop(0, groups, one, 0)

    over_groups(first.start_plane)

    lane = lax.broadcasted_iota(jnp.int32, (1, own * reach), 1)
    target = lax.rem(lane, span)
    for c in range(own):
        for j in range(listed):
            here = lane // span == c * listed + j
            target += jnp.where(here, siblings[0, c, j] * span, 0)
    row = lax.broadcasted_iota(jnp.int32, (rows, own * reach), 0)
    placing[...] = jnp.where(row == target, 1.0, 0.0).astype(jnp.bfloat16)

    def line(g):
        first.wait_plane(g)
        first.start_line(g)

    over_groups(line)

    taken = pieces.shape[3] // own
    block = taken // (2 * n_dp)
    step = n_seq * block
    for xs in range(RING):
        for zs in range(RING):
            starts = [
                d * step + (xs * PLANE + ys * RING + zs) * block
                for d in range(n_dp)
                for ys in range(2)
            ]
            cut = [s_ref[c, :, at : at + block] for c in range(own) for at in starts]
            pieces[xs, zs] = jnp.concatenate(cut, axis=1)
    hidden[me] = pieces[x, z]

    def push_summary(i, carry):
        peer = lax.rem(me + i, n_seq)
        remote(
            pieces.at[peer // PLANE, lax.rem(peer, RING)],
            hidden.at[me],
            {"seq": peer},
            summary_send.at[0],
            summary_recv.at[0],
        ).start()
        return carry

    for load in loads:
        load.wait()

    def attend(g, c):
        keys, values = k_rows[...], v_rows[...]
        keys_t = keys.T
        size = min(PART, tokens)
        parts = [(r, t) for r in range(heads) for t in range(0, tokens, size)]
        across = (((1,), (1,)), ((), ()))

        def pick(ref, r, t):
            return ref[g, c, t : t + size, r * HEAD : (r + 1) * HEAD]

        def ahead(r, t):
            return (
                lax.dot_general(
                    keys, pick(q_all, r, t), across, preferred_element_type=jnp.float32
                ),
                lax.dot_general(
                    values, pick(do_all, r, t), across, preferred_element_type=jnp.float32
                ),
            )

        def behind(r, t, prob_half, score_half):
            value_term = jnp.dot(
                prob_half, pick(do_all, r, t), preferred_element_type=jnp.float32
            )
            key_term = jnp.dot(score_half, pick(q_all, r, t), preferred_element_type=jnp.float32)
            if (r, t) == (0, 0):
                key_acc[...] = key_term
                value_acc[...] = value_term
            else:
                key_acc[...] += key_term
                value_acc[...] += value_term
            dq_t = jnp.dot(keys_t, score_half, preferred_element_type=jnp.float32)
            dq = (dq_t * scale).astype(jnp.bfloat16).T
            dq_all[g, c, t : t + size, r * HEAD : (r + 1) * HEAD] = dq

        coming, past = ahead(*parts[0]), None
        for i, at in enumerate(parts):
            scores, prob_grad = coming
            if i + 1 < len(parts):
                coming = ahead(*parts[i + 1])
            if past is not None:
                behind(*past)
            largest = jnp.max(scores, axis=0, keepdims=True)
            exponent = jnp.exp2((scores - largest) * power)
            prob = exponent * (1.0 / jnp.sum(exponent, axis=0, keepdims=True))
            delta = jnp.sum(prob * prob_grad, axis=0, keepdims=True)
            score_half = (prob * (prob_grad - delta)).astype(jnp.bfloat16)
            past = (*at, prob.astype(jnp.bfloat16), score_half)
        behind(*past)

    def begin(c):
        for j in range(listed):
            block = kv_now[siblings[0, c, j]]
            k_rows[j * span : (j + 1) * span, :] = block[:, :HEAD]
            v_rows[j * span : (j + 1) * span, :] = block[:, HEAD:]

    def end(g, c):
        listed_grads[c * reach : (c + 1) * reach, :HEAD] = (key_acc[...] * scale).astype(jnp.bfloat16)
        listed_grads[c * reach : (c + 1) * reach, HEAD:] = value_acc[...].astype(jnp.bfloat16)
        cols = pl.ds(pl.multiple_of(g * q_block, HEAD), q_block)
        pltpu.make_async_copy(dq_all.at[g, c], dq_hbm.at[0, c, :, cols], store_sem.at[g, c]).start()

    def again_plane(g):
        summing.finish(g, again)
        again.start_plane(g)

    def again_line(g):
        again.start_line(g)

    def weigh(g):
        again.wait_line(g)
        got = 0.0
        for c in range(own):
            grads = sums[g, :, :, :, c].reshape(rows // own, HEAD)
            got += jnp.dot(hidden_t[c], grads, preferred_element_type=jnp.float32)
        product[g] = got.reshape(product.shape[1:])
        mine = me_dp * 2 + y
        shares[g, mine] = product[g, mine]
        for i in range(1, 2 * n_dp):
            d, ys = lax.rem(me_dp + i // 2, n_dp), lax.rem(y + i % 2, 2)
            remote(
                product.at[g, d * 2 + ys],
                shares.at[g, mine],
                {"dp": d, **peer_id(x, ys, z)},
                share_send.at[g],
                share_recv.at[g],
            ).start()

    def turn(it, carry):
        first.wait_line(it)
        kv_now[...] = kv[it].reshape(kv_now.shape)
        for c in range(own):
            if c == own - 1:

                @pl.when(it >= 2)
                def _():
                    summing.line_to_plane(it - 2)

            begin(c)
            attend(it, c)
            end(it, c)
        got = jnp.dot(placing[...], listed_grads[...], preferred_element_type=jnp.float32)
        part[it] = got.astype(jnp.bfloat16).reshape(part.shape[1:])
        summing.start_line(it)

        @pl.when(it == 1)
        def _():
            lax.fori_loop(1, n_seq, push_summary, 0)

        return carry

    lax.fori_loop(0, groups, turn, 0)
    wait_blocks(hidden, n_seq - 1, summary_recv.at[0])
    for c in range(own):
        columns = hidden[:, :, c * taken : (c + 1) * taken]
        hidden_t[c] = columns.reshape(rows // own, taken).T
    for g in range(groups - 2):
        again_plane(g)
    for g in range(groups - 2, groups):
        summing.line_to_plane(g)
    for g in range(groups - 2):
        again_line(g)
    for g in range(groups - 2, groups):
        again_plane(g)
    for g in range(groups):
        if g < 2:
            again_line(groups - 2 + g)
        weigh(g)
    half = out_ref.shape[1] // 2
    for g in range(groups):
        wait_blocks(shares.at[g], 2 * n_dp - 1, share_recv.at[g])
        for ys in range(2):
            result = shares[g, ys]
            for d in range(1, n_dp):
                result = result + shares[g, 2 * d + ys]
            out_ref[:, ys * half + g * HEAD : ys * half + (g + 1) * HEAD] = result

    def drain(g):
        first.wait_sent(g)
        again.wait_sent(g)
        summing.wait_sent(g)
        wait_blocks(shares.at[g], 2 * n_dp - 1, share_send.at[g])
        for c in range(own):
            pltpu.make_async_copy(
                dq_all.at[g, c], dq_hbm.at[0, c, :, pl.ds(0, q_block)], store_sem.at[g, c]
            ).wait()

    over_groups(drain)
    wait_blocks(hidden, n_seq - 1, summary_send.at[0])


def per_device(n_dp, n_seq, siblings, queries, grad_out, keys_in, input_values, summary):
    _, own, tokens, q_width = queries.shape
    span, kv_width = keys_in.shape[2], keys_in.shape[3]
    listed = siblings.shape[2]
    groups = kv_width // HEAD
    q_block = q_width // groups
    rows = own * span
    everyone = n_seq * rows
    block = summary.shape[3] // (n_dp * n_seq)
    any_space = pl.BlockSpec(memory_space=pl.ANY)
    vmem = pl.BlockSpec(memory_space=pltpu.VMEM)
    smem = pl.BlockSpec(memory_space=pltpu.SMEM)
    half = jnp.bfloat16
    tile, thin = (span, 2 * HEAD), (span, HEAD)
    taken = 2 * n_dp * block
    whole = pltpu.VMEM((groups, RING, 2, RING, own, *tile), half)
    tokens_all = pltpu.VMEM((groups, own, tokens, q_block), half)
    shares = pltpu.VMEM((groups, 2 * n_dp, block, HEAD), jnp.float32)
    pairs = pltpu.SemaphoreType.DMA((groups, 2))
    return pl.pallas_call(
        functools.partial(kernel, n_seq, n_dp),
        out_shape=(
            jax.ShapeDtypeStruct(queries.shape, half),
            jax.ShapeDtypeStruct((block, 2 * kv_width), jnp.float32),
        ),
        in_specs=[smem, vmem, vmem, vmem, any_space, any_space],
        out_specs=(any_space, vmem),
        scratch_shapes=[
            tokens_all,
            tokens_all,
            tokens_all,
            whole,
            pltpu.VMEM((n_seq * own, *tile), half),
            pltpu.VMEM((listed * span, HEAD), half),
            pltpu.VMEM((listed * span, HEAD), half),
            pltpu.VMEM((listed * span, HEAD), jnp.float32),
            pltpu.VMEM((listed * span, HEAD), jnp.float32),
            pltpu.VMEM((own * listed * span, 2 * HEAD), half),
            pltpu.VMEM((everyone, own * listed * span), half),
            whole,
            pltpu.VMEM((groups, RING - 1, 2, RING, *tile), half),
            pltpu.VMEM((groups, RING - 1, RING, 2, *tile), half),
            pltpu.VMEM((groups, 2, RING, *tile), half),
            pltpu.VMEM((groups, RING, 2, *tile), half),
            pltpu.VMEM((groups, 2, PLANE - 1, *tile), half),
            pltpu.VMEM((groups, 2, own, *thin), half),
            pltpu.VMEM((groups, RING, 2, RING, own, *thin), half),
            pltpu.VMEM((RING, RING, span, own * taken), half),
            pltpu.VMEM((n_seq, span, own * taken), half),
            pltpu.VMEM((own, taken, everyone // own), half),
            shares,
            shares,
            pltpu.VMEM((2 * (RING - 1) * PLANE, *tile), half),
            pltpu.SemaphoreType.DMA((2, groups, own)),
            pltpu.SemaphoreType.DMA((groups, own)),
            *[pairs] * 6,
            pltpu.SemaphoreType.DMA((groups,)),
            pltpu.SemaphoreType.DMA((groups,)),
            pltpu.SemaphoreType.DMA((1,)),
            pltpu.SemaphoreType.DMA((1,)),
        ],
        compiler_params=pltpu.CompilerParams(
            collective_id=0, has_side_effects=True, vmem_limit_bytes=LIMIT
        ),
    )(siblings, keys_in[0], input_values[0], summary[0], queries, grad_out)


def solution(mesh):
    placed = (
        P("dp", "seq", None),
        P("dp", "seq", None, None),
        P("dp", "seq", None, None),
        P("dp", "seq", None, None),
        P("dp", "seq", None, None),
        P("dp", "seq", None, None),
    )
    return jax.shard_map(
        functools.partial(per_device, mesh.shape["dp"], mesh.shape["seq"]),
        mesh=mesh,
        in_specs=placed,
        out_specs=(P("dp", "seq", None, None), P(("dp", "seq"), None)),
        check_vma=False,
    )
```

```python
import functools
import math

import jax
import jax.numpy as jnp
from jax import lax
from jax.experimental import pallas as pl
from jax.experimental.pallas import tpu as pltpu
from jax.sharding import PartitionSpec as P

HEAD = 128
MESH = pl.DeviceIdType.MESH
LIMIT = 56 * 1024 * 1024
RING = 4
PART = 256
PLANE = 2 * RING


def signal_peers(barrier, axis, me, count):
    def one(i, carry):
        pl.semaphore_signal(
            barrier,
            inc=1,
            device_id={axis: lax.rem(me + i, count)},
            device_id_type=MESH,
        )
        return carry

    lax.fori_loop(1, count, one, 0)


def wait_blocks(ref, count, sem):
    part = ref.at[pl.ds(0, count)]
    pltpu.make_async_copy(part, part, sem).wait()


def wide(value):
    return value.astype(jnp.float32)


def ring(at, shift):
    return lax.rem(at + shift, RING)


def place():
    me = lax.axis_index("seq")
    return me // PLANE, lax.rem(me // RING, 2), lax.rem(me, RING)


def peer_id(x, y, z):
    return {"seq": x * PLANE + y * RING + z}


def remote(src, dst, peer, send_sem, recv_sem):
    return pltpu.make_async_remote_copy(
        src_ref=src,
        dst_ref=dst,
        send_sem=send_sem,
        recv_sem=recv_sem,
        device_id=peer,
        device_id_type=MESH,
    )


def plane_shifts():
    return [(1, 2), (1, 1), (1, 3), (0, 2), (1, 0), (0, 1), (0, 3)]


class Spread:
    def __init__(self, buf, ruler, send_sem, recv_sem):
        self.buf, self.ruler = buf, ruler
        self.send_sem, self.recv_sem = send_sem, recv_sem

    def start_plane(self, g):
        x, y, z = place()
        for dy, shift in plane_shifts():
            other = lax.rem(y + dy, 2)
            for half, peer in (
                (0, peer_id(x, other, ring(z, shift))),
                (1, peer_id(ring(x, shift), other, z)),
            ):
                block = self.buf.at[g, x, y, z, half]
                remote(block, block, peer, self.send_sem.at[g, 0], self.recv_sem.at[g, 0]).start()

    def wait_plane(self, g):
        wait_blocks(self.ruler, 2 * (PLANE - 1), self.recv_sem.at[g, 0])

    def start_line(self, g):
        x, y, z = place()
        for shift in (2, 1, 3):
            first = self.buf.at[g, x, :, :, 0]
            second = self.buf.at[g, :, :, z, 1]
            sems = (self.send_sem.at[g, 1], self.recv_sem.at[g, 1])
            remote(first, first, peer_id(ring(x, shift), y, z), *sems).start()
            remote(second, second, peer_id(x, y, ring(z, shift)), *sems).start()

    def wait_line(self, g):
        wait_blocks(self.ruler, 2 * (RING - 1) * PLANE, self.recv_sem.at[g, 1])

    def wait_sent(self, g):
        wait_blocks(self.ruler, 2 * (PLANE - 1), self.send_sem.at[g, 0])
        wait_blocks(self.ruler, 2 * (RING - 1) * PLANE, self.send_sem.at[g, 1])


class Halves:
    def __init__(self, own, buf, ruler, send_sem, recv_sem):
        self.own, self.buf, self.ruler = own, buf, ruler
        self.send_sem, self.recv_sem = send_sem, recv_sem

    def start_plane(self, g):
        x, y, z = place()
        self.buf[g, x, y, z] = self.own[g, y]
        sems = (self.send_sem.at[g, 0], self.recv_sem.at[g, 0])
        for dy, shift in plane_shifts():
            other = lax.rem(y + dy, 2)
            for half, peer in (
                (0, peer_id(x, other, ring(z, shift))),
                (1, peer_id(ring(x, shift), other, z)),
            ):
                remote(
                    self.own.at[g, other, half], self.buf.at[g, x, y, z, half], peer, *sems
                ).start()

    def start_line(self, g):
        x, y, z = place()
        wait_blocks(self.ruler, PLANE - 1, self.recv_sem.at[g, 0])
        sems = (self.send_sem.at[g, 1], self.recv_sem.at[g, 1])
        for shift in (2, 1, 3):
            first = self.buf.at[g, x, :, :, 0]
            second = self.buf.at[g, :, :, z, 1]
            remote(first, first, peer_id(ring(x, shift), y, z), *sems).start()
            remote(second, second, peer_id(x, y, ring(z, shift)), *sems).start()

    def wait_line(self, g):
        wait_blocks(self.ruler, (RING - 1) * PLANE, self.recv_sem.at[g, 1])

    def wait_sent(self, g):
        wait_blocks(self.ruler, PLANE - 1, self.send_sem.at[g, 0])
        wait_blocks(self.ruler, (RING - 1) * PLANE, self.send_sem.at[g, 1])


class Reduce:
    def __init__(self, part, line_a, line_b, sum_a, sum_b, plane, ruler, send_sem, recv_sem):
        self.part, self.ruler = part, ruler
        self.line_a, self.line_b = line_a, line_b
        self.sum_a, self.sum_b, self.plane = sum_a, sum_b, plane
        self.send_sem, self.recv_sem = send_sem, recv_sem

    def start_line(self, g):
        x, y, z = place()
        sems = (self.send_sem.at[g, 0], self.recv_sem.at[g, 0])
        for shift in (2, 1, 3):
            xs, zs = ring(x, shift), ring(z, shift)
            slot = shift - 1
            remote(
                self.part.at[g, xs, :, :, 0], self.line_a.at[g, slot], peer_id(xs, y, z), *sems
            ).start()
            remote(
                self.part.at[g, :, :, zs, 1], self.line_b.at[g, slot], peer_id(x, y, zs), *sems
            ).start()

    def line_to_plane(self, g):
        x, y, z = place()
        wait_blocks(self.ruler, 2 * (RING - 1) * PLANE, self.recv_sem.at[g, 0])
        total_a = wide(self.part[g, x, :, :, 0])
        total_b = wide(self.part[g, :, :, z, 1])
        for slot in range(RING - 1):
            total_a += wide(self.line_a[g, slot])
            total_b += wide(self.line_b[g, slot])
        self.sum_a[g] = total_a.astype(jnp.bfloat16)
        self.sum_b[g] = total_b.astype(jnp.bfloat16)
        sems = (self.send_sem.at[g, 1], self.recv_sem.at[g, 1])
        for i, (dy, shift) in enumerate(plane_shifts()):
            other, xs, zs = lax.rem(y + dy, 2), ring(x, shift), ring(z, shift)
            remote(
                self.sum_a.at[g, other, zs], self.plane.at[g, 0, i], peer_id(x, other, zs), *sems
            ).start()
            remote(
                self.sum_b.at[g, xs, other], self.plane.at[g, 1, i], peer_id(xs, other, z), *sems
            ).start()

    def finish(self, g, out):
        x, y, z = place()
        wait_blocks(self.ruler, 2 * (PLANE - 1), self.recv_sem.at[g, 1])
        for half, own in ((0, self.sum_a[g, y, z]), (1, self.sum_b[g, x, y])):
            total = wide(own)
            for i in range(PLANE - 1):
                total += wide(self.plane[g, half, i])
            total = total.astype(jnp.bfloat16)
            for which in range(2):
                out.own[g, which, half] = total[:, which * HEAD : (which + 1) * HEAD]

    def wait_sent(self, g):
        wait_blocks(self.ruler, 2 * (RING - 1) * PLANE, self.send_sem.at[g, 0])
        wait_blocks(self.ruler, 2 * (PLANE - 1), self.send_sem.at[g, 1])


def kernel(
    n_seq,
    n_dp,
    siblings,
    k_ref,
    v_ref,
    s_ref,
    q_hbm,
    do_hbm,
    dq_hbm,
    out_ref,
    q_all,
    do_all,
    dq_all,
    kv,
    kv_now,
    k_rows,
    v_rows,
    score_all,
    key_acc,
    value_acc,
    listed_grads,
    placing,
    part,
    line_a,
    line_b,
    sum_a,
    sum_b,
    plane,
    sum_own,
    sums,
    pieces,
    hidden,
    hidden_t,
    product,
    shares,
    ruler,
    load_sem,
    store_sem,
    spread_send,
    spread_recv,
    reduce_send,
    reduce_recv,
    again_send,
    again_recv,
    share_send,
    share_recv,
    summary_send,
    summary_recv,
):
    me, me_dp = lax.axis_index("seq"), lax.axis_index("dp")
    x, y, z = place()
    groups, own, tokens, q_block = q_all.shape
    heads = q_block // HEAD
    span = k_ref.shape[1]
    listed = siblings.shape[2]
    reach = listed * span
    rows = n_seq * own * span
    scale = 1.0 / math.sqrt(HEAD)
    power = scale * math.log2(math.e)

    barrier = pltpu.get_barrier_semaphore()
    signal_peers(barrier, "seq", me, n_seq)
    for i in range(1, n_dp):
        for across_y in range(2):
            pl.semaphore_signal(
                barrier,
                inc=1,
                device_id={"dp": lax.rem(me_dp + i, n_dp), **peer_id(x, across_y, z)},
                device_id_type=MESH,
            )
    loads = []
    for g in range(groups):
        cols = pl.ds(g * q_block, q_block)
        for c in range(own):
            loads.append(pltpu.make_async_copy(q_hbm.at[0, c, :, cols], q_all.at[g, c], load_sem.at[0, g, c]))
            loads.append(pltpu.make_async_copy(do_hbm.at[0, c, :, cols], do_all.at[g, c], load_sem.at[1, g, c]))
    for load in loads:
        load.start()
    for g in range(groups):
        cols = slice(g * HEAD, (g + 1) * HEAD)
        kv[g, x, y, z, :, :, :HEAD] = k_ref[:, :, cols]
        kv[g, x, y, z, :, :, HEAD:] = v_ref[:, :, cols]
    pl.semaphore_wait(barrier, n_seq - 1 + 2 * (n_dp - 1))

    first = Spread(kv, ruler, spread_send, spread_recv)
    again = Halves(sum_own, sums, ruler, again_send, again_recv)
    summing = Reduce(part, line_a, line_b, sum_a, sum_b, plane, ruler, reduce_send, reduce_recv)

    def over_groups(step):
        def one(g, carry):
            step(g)
            return carry

        lax.fori_loop(0, groups, one, 0)

    over_groups(first.start_plane)

    lane = lax.broadcasted_iota(jnp.int32, (1, own * reach), 1)
    target = lax.rem(lane, span)
    for c in range(own):
        for j in range(listed):
            here = lane // span == c * listed + j
            target += jnp.where(here, siblings[0, c, j] * span, 0)
    row = lax.broadcasted_iota(jnp.int32, (rows, own * reach), 0)
    placing[...] = jnp.where(row == target, 1.0, 0.0).astype(jnp.bfloat16)

    def line(g):
        first.wait_plane(g)
        first.start_line(g)

    over_groups(line)

    taken = pieces.shape[3] // own
    block = taken // (2 * n_dp)
    step = n_seq * block
    for xs in range(RING):
        for zs in range(RING):
            starts = [
                d * step + (xs * PLANE + ys * RING + zs) * block
                for d in range(n_dp)
                for ys in range(2)
            ]
            cut = [s_ref[c, :, at : at + block] for c in range(own) for at in starts]
            pieces[xs, zs] = jnp.concatenate(cut, axis=1)
    hidden[me] = pieces[x, z]

    def push_summary(i, carry):
        peer = lax.rem(me + i, n_seq)
        remote(
            pieces.at[peer // PLANE, lax.rem(peer, RING)],
            hidden.at[me],
            {"seq": peer},
            summary_send.at[0],
            summary_recv.at[0],
        ).start()
        return carry


    def attend(g, c):
        keys, values = k_rows[g, c], v_rows[...]
        size = min(PART, tokens)
        parts = [(r, t) for r in range(heads) for t in range(0, tokens, size)]
        across = (((1,), (1,)), ((), ()))

        def pick(ref, r, t):
            return ref[g, c, t : t + size, r * HEAD : (r + 1) * HEAD]

        def ahead(r, t):
            return (
                lax.dot_general(
                    keys, pick(q_all, r, t), across, preferred_element_type=jnp.float32
                ),
                lax.dot_general(
                    values, pick(do_all, r, t), across, preferred_element_type=jnp.float32
                ),
            )

        def behind(r, t, prob_half, score_half):
            value_term = jnp.dot(
                prob_half, pick(do_all, r, t), preferred_element_type=jnp.float32
            )
            key_term = jnp.dot(score_half, pick(q_all, r, t), preferred_element_type=jnp.float32)
            if (r, t) == (0, 0):
                key_acc[...] = key_term
                value_acc[...] = value_term
            else:
                key_acc[...] += key_term
                value_acc[...] += value_term
            score_all[g, c, :, r * tokens + t : r * tokens + t + size] = score_half

        coming, past = ahead(*parts[0]), None
        for i, at in enumerate(parts):
            scores, prob_grad = coming
            if i + 1 < len(parts):
                coming = ahead(*parts[i + 1])
            if past is not None:
                behind(*past)
            largest = jnp.max(scores, axis=0, keepdims=True)
            exponent = jnp.exp2((scores - largest) * power)
            prob = exponent * (1.0 / jnp.sum(exponent, axis=0, keepdims=True))
            delta = jnp.sum(prob * prob_grad, axis=0, keepdims=True)
            score_half = (prob * (prob_grad - delta)).astype(jnp.bfloat16)
            past = (*at, prob.astype(jnp.bfloat16), score_half)
        behind(*past)

    def begin(g, c):
        for j in range(listed):
            block = kv_now[siblings[0, c, j]]
            k_rows[g, c, j * span : (j + 1) * span, :] = block[:, :HEAD]
            v_rows[j * span : (j + 1) * span, :] = block[:, HEAD:]

    def end(g, c):
        listed_grads[c * reach : (c + 1) * reach, :HEAD] = (key_acc[...] * scale).astype(jnp.bfloat16)
        listed_grads[c * reach : (c + 1) * reach, HEAD:] = value_acc[...].astype(jnp.bfloat16)

    def query_gradient(g):
        def one(c, carry):
            keys_t = k_rows[g, c].T
            for r in range(heads):
                scores = score_all[g, c, :, r * tokens : (r + 1) * tokens]
                dq_t = jnp.dot(keys_t, scores, preferred_element_type=jnp.float32)
                dq_all[g, c, :, r * HEAD : (r + 1) * HEAD] = (dq_t * scale).astype(jnp.bfloat16).T
            cols = pl.ds(g * q_block, q_block)
            pltpu.make_async_copy(
                dq_all.at[g, c], dq_hbm.at[0, c, :, cols], store_sem.at[g, c]
            ).start()
            return carry

        lax.fori_loop(0, own, one, 0)

    def again_plane(g):
        summing.finish(g, again)
        again.start_plane(g)

    def again_line(g):
        again.start_line(g)

    def weigh(g):
        again.wait_line(g)
        got = 0.0
        for c in range(own):
            grads = sums[g, :, :, :, c].reshape(rows // own, HEAD)
            got += jnp.dot(hidden_t[c], grads, preferred_element_type=jnp.float32)
        product[g] = got.reshape(product.shape[1:])
        mine = me_dp * 2 + y
        shares[g, mine] = product[g, mine]
        for i in range(1, 2 * n_dp):
            d, ys = lax.rem(me_dp + i // 2, n_dp), lax.rem(y + i % 2, 2)
            remote(
                product.at[g, d * 2 + ys],
                shares.at[g, mine],
                {"dp": d, **peer_id(x, ys, z)},
                share_send.at[g],
                share_recv.at[g],
            ).start()

    def turn(it, carry):
        first.wait_line(it)
        kv_now[...] = kv[it].reshape(kv_now.shape)
        for c in range(own):
            if c == own - 1:

                @pl.when(it >= 2)
                def _():
                    summing.line_to_plane(it - 2)

            begin(it, c)
            for kind, ref in ((0, q_all), (1, do_all)):
                pltpu.make_async_copy(ref.at[it, c], ref.at[it, c], load_sem.at[kind, it, c]).wait()
            attend(it, c)
            end(it, c)
        got = jnp.dot(placing[...], listed_grads[...], preferred_element_type=jnp.float32)
        part[it] = got.astype(jnp.bfloat16).reshape(part.shape[1:])
        summing.start_line(it)

        @pl.when(it == 1)
        def _():
            lax.fori_loop(1, n_seq, push_summary, 0)

        return carry

    lax.fori_loop(0, groups, turn, 0)
    last = groups - 1
    for g in range(groups - 2):
        again_plane(g)
    summing.line_to_plane(last - 1)
    query_gradient(0)
    summing.line_to_plane(last)
    for g in range(groups - 2):
        again_line(g)
    again_plane(last - 1)
    wait_blocks(hidden, n_seq - 1, summary_recv.at[0])
    for c in range(own):
        columns = hidden[:, :, c * taken : (c + 1) * taken]
        hidden_t[c] = columns.reshape(rows // own, taken).T
    query_gradient(1)
    again_plane(last)
    again_line(last - 1)
    weigh(0)
    query_gradient(last - 1)
    again_line(last)
    weigh(1)
    weigh(last - 1)
    query_gradient(last)
    weigh(last)
    half = out_ref.shape[1] // 2
    for g in range(groups):
        wait_blocks(shares.at[g], 2 * n_dp - 1, share_recv.at[g])
        for ys in range(2):
            result = shares[g, ys]
            for d in range(1, n_dp):
                result = result + shares[g, 2 * d + ys]
            out_ref[:, ys * half + g * HEAD : ys * half + (g + 1) * HEAD] = result

    def drain(g):
        first.wait_sent(g)
        again.wait_sent(g)
        summing.wait_sent(g)
        wait_blocks(shares.at[g], 2 * n_dp - 1, share_send.at[g])
        for c in range(own):
            pltpu.make_async_copy(
                dq_all.at[g, c], dq_hbm.at[0, c, :, pl.ds(0, q_block)], store_sem.at[g, c]
            ).wait()

    over_groups(drain)
    wait_blocks(hidden, n_seq - 1, summary_send.at[0])


def per_device(n_dp, n_seq, siblings, queries, grad_out, keys_in, input_values, summary):
    _, own, tokens, q_width = queries.shape
    span, kv_width = keys_in.shape[2], keys_in.shape[3]
    listed = siblings.shape[2]
    groups = kv_width // HEAD
    q_block = q_width // groups
    heads = q_block // HEAD
    rows = own * span
    everyone = n_seq * rows
    block = summary.shape[3] // (n_dp * n_seq)
    any_space = pl.BlockSpec(memory_space=pl.ANY)
    vmem = pl.BlockSpec(memory_space=pltpu.VMEM)
    smem = pl.BlockSpec(memory_space=pltpu.SMEM)
    half = jnp.bfloat16
    tile, thin = (span, 2 * HEAD), (span, HEAD)
    taken = 2 * n_dp * block
    whole = pltpu.VMEM((groups, RING, 2, RING, own, *tile), half)
    tokens_all = pltpu.VMEM((groups, own, tokens, q_block), half)
    shares = pltpu.VMEM((groups, 2 * n_dp, block, HEAD), jnp.float32)
    pairs = pltpu.SemaphoreType.DMA((groups, 2))
    return pl.pallas_call(
        functools.partial(kernel, n_seq, n_dp),
        out_shape=(
            jax.ShapeDtypeStruct(queries.shape, half),
            jax.ShapeDtypeStruct((block, 2 * kv_width), jnp.float32),
        ),
        in_specs=[smem, vmem, vmem, vmem, any_space, any_space],
        out_specs=(any_space, vmem),
        scratch_shapes=[
            tokens_all,
            tokens_all,
            tokens_all,
            whole,
            pltpu.VMEM((n_seq * own, *tile), half),
            pltpu.VMEM((groups, own, listed * span, HEAD), half),
            pltpu.VMEM((listed * span, HEAD), half),
            pltpu.VMEM((groups, own, listed * span, heads * tokens), half),
            pltpu.VMEM((listed * span, HEAD), jnp.float32),
            pltpu.VMEM((listed * span, HEAD), jnp.float32),
            pltpu.VMEM((own * listed * span, 2 * HEAD), half),
            pltpu.VMEM((everyone, own * listed * span), half),
            whole,
            pltpu.VMEM((groups, RING - 1, 2, RING, *tile), half),
            pltpu.VMEM((groups, RING - 1, RING, 2, *tile), half),
            pltpu.VMEM((groups, 2, RING, *tile), half),
            pltpu.VMEM((groups, RING, 2, *tile), half),
            pltpu.VMEM((groups, 2, PLANE - 1, *tile), half),
            pltpu.VMEM((groups, 2, own, *thin), half),
            pltpu.VMEM((groups, RING, 2, RING, own, *thin), half),
            pltpu.VMEM((RING, RING, span, own * taken), half),
            pltpu.VMEM((n_seq, span, own * taken), half),
            pltpu.VMEM((own, taken, everyone // own), half),
            shares,
            shares,
            pltpu.VMEM((2 * (RING - 1) * PLANE, *tile), half),
            pltpu.SemaphoreType.DMA((2, groups, own)),
            pltpu.SemaphoreType.DMA((groups, own)),
            *[pairs] * 6,
            pltpu.SemaphoreType.DMA((groups,)),
            pltpu.SemaphoreType.DMA((groups,)),
            pltpu.SemaphoreType.DMA((1,)),
            pltpu.SemaphoreType.DMA((1,)),
        ],
        compiler_params=pltpu.CompilerParams(
            collective_id=0, has_side_effects=True, vmem_limit_bytes=LIMIT
        ),
    )(siblings, keys_in[0], input_values[0], summary[0], queries, grad_out)


def solution(mesh):
    placed = (
        P("dp", "seq", None),
        P("dp", "seq", None, None),
        P("dp", "seq", None, None),
        P("dp", "seq", None, None),
        P("dp", "seq", None, None),
        P("dp", "seq", None, None),
    )
    return jax.shard_map(
        functools.partial(per_device, mesh.shape["dp"], mesh.shape["seq"]),
        mesh=mesh,
        in_specs=placed,
        out_specs=(P("dp", "seq", None, None), P(("dp", "seq"), None)),
        check_vma=False,
    )
```
